256 devices in a mesh: grp: 4 (over y), lane: 64 (over z, x, core).
Axes of the slice: x: 4, y: 4, z: 8, core: 2. Of those that a mesh axis runs over, the one named last changes fastest.
Arguments:
- tiles: float32 [4, 64, 48, 128, 128], P('grp', 'lane'), may hold values from -0.01953125 to 0.01953125
- tile_dest: int32 [4, 64, 48, 1], P('grp', 'lane'), may hold values from 0 to 63; in each aligned block of 48 rows (0 to 47, 48 to 95, ..., all dimensions but the last counted through in order) no two rows name the same one
- tile_row: int32 [4, 64, 48], P('grp', 'lane'), may hold values from 0 to 1
- tile_col: int32 [4, 64, 48], P('grp', 'lane'), may hold values from 0 to 3
- omega: float32 [32768, 256], P('lane'), may hold values from -6 to 6
- col_scale: int32 [32768], P('lane'), may hold values from 1 to 4
Outputs:
- range_sketch: float32 [16384, 256], P('lane')
- corange_sketch: float32 [32768, 256], P('lane')
The draws below stay inside these ranges and needn't reach their ends.
Inputs may be any that keep to these rules, and one draw needn't show every extreme that they name: `tile_dest`: among the tiles of one device, at most 1 name the same lane index.
All inputs are finite; a program needn't handle non-finite values.
Results may differ from the reference program's by a relative error of at most 0.0001.
Values sent between devices are 32-bit elements; how exact they have to be, the bound alone decides.
No kernel may reach another device: no remote copies, remote signals or barrier semaphores. Data moves between devices by JAX's collectives and lax.ppermute only.
A program may use at most 128 MiB of HBM per device.

```python
import math
import jax
import jax.numpy as jnp
import numpy as np
from jax import lax

TILE = 128
K = 256
TILES_DEV = 48
RT_DEV = 2
CT_DEV = 4
CAP = 1
NCOLS = 32768
N_GRP = 4
N_LANE = 64


def with_ends(result, own_key, smallest, high):
    spot = [jax.random.randint(jax.random.fold_in(own_key, axis), (), 0, length) for axis, length in enumerate(result.shape)]
    main_axis = result.shape.index(max(result.shape))
    beside = spot[:main_axis] + [(spot[main_axis] + 1) % result.shape[main_axis]] + spot[main_axis + 1:]
    return result.at[tuple(spot)].set(smallest).at[tuple(beside)].set(high)


def levels(rng, extent, shards, least, top_value):
    level = 1.0
    for position, blocks in shards:
        steps = jax.random.uniform(jax.random.fold_in(jax.random.fold_in(rng, 6), position), (blocks,), jnp.float32, least / len(shards), top_value / len(shards))
        level = level * jnp.repeat(jnp.exp(steps), extent[position] // blocks).reshape((-1,) + (1,) * (len(extent) - 1 - position))
    return level


def routed_block(rng, own, number, rows, number_of, top, limit, skew):
    sequence = jax.random.permutation(rng, number_of)
    heavy_load, usual = load_shares(number_of, rows * top, limit, skew, True), load_shares(number_of, rows * top, limit, skew, False)
    places = jnp.arange(number_of)

    def named(sizes, rotation):
        used = int((sizes > 0).sum())
        fixed = max(1, used // 4)
        shifted = fixed + (places - fixed + rotation * (used - fixed)) % max(1, number_of - fixed)
        return jnp.zeros((number_of,), jnp.int32).at[sequence[jnp.where(places < fixed, places, shifted)]].set(jnp.asarray(sizes, jnp.int32))

    sizes = jnp.where(number % 4 == 0, named(heavy_load, number // 4), named(usual, number - number // 4 - 1))
    mixed = jax.random.permutation(jax.random.fold_in(own, 3), number_of)
    giver, taker = mixed[0:number_of // 2 * 2:2], mixed[1:number_of // 2 * 2:2]
    slack = jnp.minimum(sizes[giver] - 1, limit - sizes[taker]) // 2
    slack = jnp.where((giver == sequence[0]) | (taker == sequence[0]) | (sizes[taker] == 0), 0, jnp.maximum(slack, 0))
    shifted = jax.random.randint(jax.random.fold_in(own, 4), (number_of // 2,), 0, 1 << 20) % (slack + 1)
    sizes = sizes.at[giver].add(-shifted).at[taker].add(shifted)
    items = jnp.searchsorted(jnp.cumsum(sizes), jnp.arange(rows * top), side="right").astype(jnp.int32)
    table = items.reshape(top, rows).T
    table = table[jax.random.permutation(jax.random.fold_in(own, 1), rows)]
    rotation = jax.random.randint(jax.random.fold_in(own, 2), (rows, 1), 0, top)
    return jnp.take_along_axis(table, (jnp.arange(top)[None, :] + rotation) % top, axis=1)


def load_shares(count, total, most, slope, full):
    loads = [(1 << 20) // math.isqrt(rank ** slope) + 1 for rank in range(1, count + 1)]
    largest = most if full else min(most, max(-(-total // count), total * loads[0] // sum(loads)))
    least = 1 if total - largest >= count - 1 else 0
    counts, surplus = [largest] + [least] * (count - 1), total - largest - least * (count - 1)
    while surplus > 0:
        candidates = [i for i in range(1, count) if counts[i] < largest] or [i for i in range(1, count) if counts[i] < most]
        whole, left = sum([loads[i] for i in candidates]), surplus
        for i in candidates:
            more = min(most - counts[i], max(1, left * loads[i] // whole), surplus)
            counts[i] = counts[i] + more
            surplus = surplus - more
    return np.array(counts)


def gaussian(own_key, dims, spread, most, split=(), kind=jnp.bfloat16):
    entries = spread * jax.random.normal(own_key, dims, jnp.float32)
    if split:
        entries = entries * levels(own_key, dims, split, -0.22, 0.18)
    return jnp.clip(entries, -most, most).astype(kind)


def setup_inputs(seed: int = 0) -> dict:
    splits = jax.random.split(jax.random.key(seed), 7)
    tiles = gaussian(splits[0], (N_GRP, N_LANE, TILES_DEV, TILE, TILE), (8 * TILE * TILES_DEV * N_GRP // RT_DEV) ** -0.5, 0.01953125, ((0, 4), (1, 64)), jnp.float32)
    tile_dest_keys = jax.random.split(jax.random.fold_in(splits[1], 1), N_GRP * N_LANE * TILES_DEV // TILES_DEV)
    tile_dest_turns = jax.random.permutation(jax.random.fold_in(splits[1], 3), N_GRP * N_LANE * TILES_DEV // TILES_DEV)
    tile_dest = jax.vmap(lambda own, number: routed_block(jax.random.fold_in(splits[1], 2), own, number, TILES_DEV, N_LANE, 1, CAP, 2))(tile_dest_keys, tile_dest_turns).reshape((N_GRP, N_LANE, TILES_DEV, 1))
    tile_row = with_ends(jax.random.randint(splits[2], (N_GRP, N_LANE, TILES_DEV), 0, RT_DEV), jax.random.fold_in(splits[2], 1), 0, RT_DEV - 1).astype(jnp.int32)
    tile_col = with_ends(jax.random.randint(splits[3], (N_GRP, N_LANE, TILES_DEV), 0, CT_DEV), jax.random.fold_in(splits[3], 1), 0, CT_DEV - 1).astype(jnp.int32)
    omega = gaussian(splits[4], (NCOLS, K), 1.0, 6.0, ((0, 64),), jnp.float32)
    col_scale = with_ends(jax.random.randint(splits[5], (NCOLS,), 1, 5), jax.random.fold_in(splits[5], 1), 1, 4).astype(jnp.int32)
    return {"tiles": tiles, "tile_dest": tile_dest, "tile_row": tile_row, "tile_col": tile_col, "omega": omega, "col_scale": col_scale}


def reference(tiles, tile_dest, tile_row, tile_col, omega, col_scale):
    highest = lax.Precision.HIGHEST
    weights = col_scale.astype(jnp.float32)
    scaled = (omega * weights[:, None]).reshape(-1, TILE, K)
    lane_ids = jnp.arange(N_LANE, dtype=jnp.int32)[None, :, None]
    grow = (tile_dest[..., 0] * RT_DEV + tile_row).reshape(-1, TILES_DEV).astype(jnp.int32)
    gcol = (lane_ids * CT_DEV + tile_col).reshape(-1, TILES_DEV).astype(jnp.int32)
    blocks = tiles.reshape(-1, TILES_DEV, TILE, TILE)

    def add_range(total, item):
        block, rows, cols = item
        part = jnp.einsum("tij,tjk->tik", block, scaled[cols], precision=highest)
        return total.at[rows].add(part), None

    start_y = jnp.zeros((RT_DEV * N_LANE, TILE, K), jnp.float32)
    range_tiles, _ = lax.scan(add_range, start_y, (blocks, grow, gcol))

    def add_corange(total, item):
        block, rows, cols = item
        part = jnp.einsum("tij,tik->tjk", block, range_tiles[rows], precision=highest)
        return total.at[cols].add(part), None

    start_z = jnp.zeros((CT_DEV * N_LANE, TILE, K), jnp.float32)
    corange_tiles, _ = lax.scan(add_corange, start_z, (blocks, grow, gcol))
    range_sketch = range_tiles.reshape(-1, K)
    corange_sketch = corange_tiles.reshape(-1, K) * weights[:, None]
    return range_sketch, corange_sketch
```

```python
import functools

import jax
import jax.numpy as jnp
from jax import lax
from jax.experimental import pallas as pl
from jax.experimental.pallas import tpu as pltpu
from jax.sharding import Mesh, PartitionSpec as P

SIDE = 128
WIDTH = 256
RT_DEV = 2
CT_DEV = 4
PER = 8
ROWS = PER * SIDE + 8
VMEM = 48 * 1024 * 1024


def split(value):
    high = value.astype(jnp.bfloat16)
    low = (value - high.astype(jnp.float32)).astype(jnp.bfloat16)
    return high, low


def dot3(a_high, a_low, b_high, b_low, contract):
    dims = (((contract,), (0,)), ((), ()))
    dot = functools.partial(
        lax.dot_general, dimension_numbers=dims, preferred_element_type=jnp.float32
    )
    return dot(a_high, b_high) + (dot(a_high, b_low) + dot(a_low, b_high))


def pack_kernel(place_ref, tiles_ref, notes_ref, out_ref, sem, note_sem):
    count = tiles_ref.shape[0]

    def tile_copy(t):
        start = pl.multiple_of(place_ref[t], 8)
        return pltpu.make_async_copy(tiles_ref.at[t], out_ref.at[pl.ds(start, SIDE)], sem.at[t])

    def note_copy(d):
        return pltpu.make_async_copy(
            notes_ref.at[d], out_ref.at[pl.ds(d * ROWS + PER * SIDE, 8)], note_sem.at[d]
        )

    for t in range(count):
        tile_copy(t).start()
    for d in range(8):
        note_copy(d).start()
    for t in range(count):
        tile_copy(t).wait()
    for d in range(8):
        note_copy(d).wait()


def pack(place, tiles, notes):
    count = tiles.shape[0]
    return pl.pallas_call(
        pack_kernel,
        out_shape=jax.ShapeDtypeStruct((8 * ROWS, SIDE), jnp.float32),
        in_specs=[
            pl.BlockSpec(memory_space=pltpu.SMEM),
            pl.BlockSpec(memory_space=pl.ANY),
            pl.BlockSpec(memory_space=pl.ANY),
        ],
        out_specs=pl.BlockSpec(memory_space=pl.ANY),
        scratch_shapes=[pltpu.SemaphoreType.DMA((count,)), pltpu.SemaphoreType.DMA((8,))],
    )(place, tiles, notes)


def range_kernel(note_ref, core_ref, msg_ref, own_ref, other_ref, out_ref, high_ref, low_ref):
    d = pl.program_id(0)

    @pl.when(d == 0)
    def _():
        out_ref[...] = jnp.zeros_like(out_ref)
        for i, ref in enumerate((own_ref, other_ref)):
            high, low = split(ref[...])
            high_ref[pl.ds(i * CT_DEV, CT_DEV)] = high
            low_ref[pl.ds(i * CT_DEV, CT_DEV)] = low

    base = jnp.where(lax.rem(d, 2) == core_ref[0], 0, CT_DEV)
    for j in range(PER):
        note = note_ref[d * PER + j]

        @pl.when(note >= 0)
        def _():
            row = j * RT_DEV + lax.div(note, CT_DEV)
            col = base + lax.rem(note, CT_DEV)
            high, low = split(msg_ref[0, pl.ds(j * SIDE, SIDE)])
            out_ref[row] += dot3(high, low, high_ref[col], low_ref[col], 1)


def range_part(notes, core, msg, own, other):
    whole = lambda n: pl.BlockSpec((n, SIDE, WIDTH), lambda d, *_: (0, 0, 0))
    return pl.pallas_call(
        range_kernel,
        out_shape=jax.ShapeDtypeStruct((PER * RT_DEV, SIDE, WIDTH), jnp.float32),
        grid_spec=pltpu.PrefetchScalarGridSpec(
            num_scalar_prefetch=2,
            grid=(8,),
            in_specs=[
                pl.BlockSpec((1, ROWS, SIDE), lambda d, *_: (d, 0, 0)),
                whole(CT_DEV),
                whole(CT_DEV),
            ],
            out_specs=whole(PER * RT_DEV),
            scratch_shapes=[pltpu.VMEM((2 * CT_DEV, SIDE, WIDTH), jnp.bfloat16)] * 2,
        ),
        compiler_params=pltpu.CompilerParams(vmem_limit_bytes=VMEM),
    )(notes, core, msg, own, other)


def corange_kernel(note_ref, msg_ref, y_ref, out_ref, high_ref, low_ref):
    d = pl.program_id(0)

    @pl.when(d == 0)
    def _():
        out_ref[...] = jnp.zeros_like(out_ref)
        for i in range(PER * RT_DEV):
            high, low = split(y_ref[i])
            high_ref[i] = high
            low_ref[i] = low

    core = lax.rem(d, 2)
    for j in range(PER):
        note = note_ref[d * PER + j]

        @pl.when(note >= 0)
        def _():
            row = j * RT_DEV + lax.div(note, CT_DEV)
            col = lax.rem(note, CT_DEV) * 2 + core
            high, low = split(msg_ref[0, pl.ds(j * SIDE, SIDE)])
            out_ref[col] += dot3(high, low, high_ref[row], low_ref[row], 0)


def corange_part(notes, msg, y):
    whole = lambda n: pl.BlockSpec((n, SIDE, WIDTH), lambda d, *_: (0, 0, 0))
    return pl.pallas_call(
        corange_kernel,
        out_shape=jax.ShapeDtypeStruct((2 * CT_DEV, SIDE, WIDTH), jnp.float32),
        grid_spec=pltpu.PrefetchScalarGridSpec(
            num_scalar_prefetch=1,
            grid=(8,),
            in_specs=[
                pl.BlockSpec((1, ROWS, SIDE), lambda d, *_: (d, 0, 0)),
                whole(PER * RT_DEV),
            ],
            out_specs=whole(2 * CT_DEV),
            scratch_shapes=[pltpu.VMEM((PER * RT_DEV, SIDE, WIDTH), jnp.bfloat16)] * 2,
        ),
        compiler_params=pltpu.CompilerParams(vmem_limit_bytes=VMEM),
    )(notes, msg, y)


def exchange(value, axes):
    return lax.all_to_all(value, axes, split_axis=0, concat_axis=0, tiled=True)


def shifted(value, axis, step):
    n = lax.axis_size(axis)
    return lax.ppermute(value, axis, [(i, (i + step) % n) for i in range(n)])


def on_device(tiles, tile_dest, tile_row, tile_col, omega, col_scale):
    blocks = tiles[0, 0]
    owner = tile_dest[0, 0, :, 0]
    y, z, core = lax.axis_index("y"), lax.axis_index("z"), lax.axis_index("c")
    weights = col_scale.astype(jnp.float32)

    dest = (owner // 8 % 4) * 2 + owner % 2
    spot = (owner // 2 % 4) * 2 + owner // 32
    hit = (dest * PER + spot)[:, None] == jnp.arange(8 * PER, dtype=jnp.int32)[None, :]
    note = tile_row[0, 0] * CT_DEV + tile_col[0, 0]
    notes = jnp.sum(jnp.where(hit, note[:, None] + 1, 0), axis=0) - 1
    notes = notes.astype(jnp.float32).reshape(8, 1, PER)
    notes = jnp.broadcast_to(jnp.pad(notes, ((0, 0), (0, 0), (0, SIDE - PER))), (8, 8, SIDE))
    packed = pack(dest * ROWS + spot * SIDE, blocks, notes)

    scaled = (omega * weights[:, None]).reshape(CT_DEV, SIDE, WIDTH)
    other = shifted(scaled, "c", 1)
    msg = exchange(packed.reshape(8, ROWS, SIDE), ("y", "c"))
    got = msg[:, PER * SIDE, :PER].reshape(8 * PER).astype(jnp.int32)

    part = range_part(got, core.reshape(1), msg, scaled, other)
    part = exchange(part, "x").reshape(4, 4 * SIDE, WIDTH).sum(axis=0)
    part = exchange(part, "z").reshape(8, 64, WIDTH).sum(axis=0)
    near = exchange(jnp.broadcast_to(part[None], (8, 64, WIDTH)), "z").reshape(512, WIDTH)
    all_rows = exchange(jnp.broadcast_to(near[None], (4, 512, WIDTH)), "x")
    all_rows = all_rows.reshape(PER * RT_DEV, SIDE, WIDTH)

    mine = lax.dynamic_slice_in_dim(near, z // 4 * 256, 256, axis=0)
    range_local = jnp.where(z % 4 == y, mine, 0.0)
    for step in range(1, 4):
        pairs = []
        for i in range(64):
            start = i // 8 % 4
            pairs.append((start * 64 + i, (start + step) % 4 * 64 + i))
        range_local = range_local + lax.ppermute(mine, ("y", "z", "x", "c"), pairs)

    columns = corange_part(got, msg, all_rows)
    columns = exchange(columns, ("y", "c")).sum(axis=0)
    owned = lax.dynamic_slice_in_dim(weights, y * SIDE, SIDE, axis=0)
    columns = columns * owned[:, None]
    parts = jnp.stack([columns] + [shifted(columns, "y", step) for step in range(1, 4)])
    order = (y - jnp.arange(4, dtype=jnp.int32)) % 4
    corange_local = jnp.take(parts, order, axis=0).reshape(CT_DEV * SIDE, WIDTH)
    return range_local, corange_local


def solution(mesh):
    fine = Mesh(mesh.devices.reshape(4, 8, 4, 2), ("y", "z", "x", "c"))
    lane = ("z", "x", "c")
    placed = (
        P("y", lane, None, None, None),
        P("y", lane, None, None),
        P("y", lane, None),
        P("y", lane, None),
        P(lane, None),
        P(lane),
    )
    return jax.shard_map(
        on_device,
        mesh=fine,
        in_specs=placed,
        out_specs=(P(lane, None), P(lane, None)),
        check_vma=False,
    )
```

```python
import jax
import jax.numpy as jnp
from jax import lax
from jax.experimental import pallas as pl
from jax.experimental.pallas import tpu as pltpu
from jax.sharding import Mesh, PartitionSpec as P

SIDE = 128
WIDTH = 256
CT_DEV = 4
NX = 4
ROWS = NX * SIDE + 8
DEPTH = 3 * SIDE
VMEM = 48 * 1024 * 1024
F32 = jnp.float32
BF16 = jnp.bfloat16


def split(value):
    high = value.astype(BF16)
    low = (value - high.astype(F32)).astype(BF16)
    return high, low


def params():
    return pltpu.CompilerParams(vmem_limit_bytes=VMEM)


def cost(flops, size):
    return pl.CostEstimate(flops=flops, bytes_accessed=size, transcendentals=0)


def pack_kernel(dest_ref, row_ref, col_ref, x_ref, tiles_ref, first_ref, second_ref, from_ref, note_ref):
    d = pl.program_id(0)

    @pl.when(d == 0)
    def _():
        for i in range(64):
            from_ref[i] = 0
            note_ref[i] = -1

        @pl.loop(0, tiles_ref.shape[0])
        def _(t):
            lane = dest_ref[t]
            z, x, c = lane // 8, lane // 2 % 4, lane % 2
            to = z % 4
            slot = (to * 2 + c) * 8 + z // 4 * 4 + (x - x_ref[0] + 4) % 4
            from_ref[slot] = t
            note_ref[slot] = row_ref[t] * CT_DEV + (col_ref[t] - to + 4) % 4

    spot = lax.broadcasted_iota(jnp.int32, (8, SIDE), 1)
    for h, ref in enumerate((first_ref, second_ref)):
        notes = jnp.full((8, SIDE), -1, jnp.int32)
        for s in range(NX):
            slot = d * 8 + h * 4 + s
            ref[0, pl.ds(s * SIDE, SIDE)] = tiles_ref[from_ref[slot]]
            notes = jnp.where(spot == s, note_ref[slot], notes)
        ref[0, pl.ds(NX * SIDE, 8)] = notes.astype(F32)


def pack(dest, row, col, x, tiles):
    smem = pl.BlockSpec(memory_space=pltpu.SMEM)
    return pl.pallas_call(
        pack_kernel,
        grid=(8,),
        out_shape=[jax.ShapeDtypeStruct((8, ROWS, SIDE), F32)] * 2,
        in_specs=[smem] * 4 + [pl.BlockSpec(tiles.shape, lambda d: (0, 0, 0))],
        out_specs=[pl.BlockSpec((1, ROWS, SIDE), lambda d: (d, 0, 0))] * 2,
        scratch_shapes=[pltpu.SMEM((64,), jnp.int32)] * 2,
        compiler_params=params(),
        name="pack",
    )(dest, row, col, x, tiles)


def stack_kernel(own_ref, other_ref, out_ref):
    for i, ref in enumerate((own_ref, other_ref)):
        for k in range(CT_DEV):
            high, low = split(ref[k])
            out_ref[i * CT_DEV + k, pl.ds(0, SIDE)] = high
            out_ref[i * CT_DEV + k, pl.ds(SIDE, SIDE)] = high
            out_ref[i * CT_DEV + k, pl.ds(2 * SIDE, SIDE)] = low


def stack(own, other):
    return pl.pallas_call(
        stack_kernel,
        out_shape=jax.ShapeDtypeStruct((2 * CT_DEV, DEPTH, WIDTH), BF16),
        compiler_params=params(),
        cost_estimate=cost(1 << 20, 3 << 20),
        name="stack",
    )(own, other)


def range_kernel(note_ref, here_ref, msg_ref, stack_ref, *out_refs):
    d = pl.program_id(0)

    @pl.when(d == 0)
    def _():
        for ref in out_refs:
            ref[...] = jnp.zeros_like(ref)

    base = jnp.where(lax.rem(d, 2) == here_ref[1], 0, CT_DEV)
    for s, ref in enumerate(out_refs):
        note = note_ref[d * NX + s]
        place = jnp.maximum(note, 0)
        col = base + (place + here_ref[0]) % CT_DEV
        tile = jnp.where(note >= 0, msg_ref[0, pl.ds(s * SIDE, SIDE)], 0.0)
        high, low = split(tile)
        left = jnp.concatenate([high, low, high], axis=1)
        ref[place // CT_DEV] += jnp.dot(left, stack_ref[col], preferred_element_type=F32)


def range_part(notes, here, msg, weights):
    return pl.pallas_call(
        range_kernel,
        out_shape=[jax.ShapeDtypeStruct((2, SIDE, WIDTH), F32)] * NX,
        grid_spec=pltpu.PrefetchScalarGridSpec(
            num_scalar_prefetch=2,
            grid=(8,),
            in_specs=[
                pl.BlockSpec((1, ROWS, SIDE), lambda d, *_: (d, 0, 0)),
                pl.BlockSpec(weights.shape, lambda d, *_: (0, 0, 0)),
            ],
            out_specs=[pl.BlockSpec((2, SIDE, WIDTH), lambda d, *_: (0, 0, 0))] * NX,
        ),
        compiler_params=params(),
        cost_estimate=cost(32 * 2 * SIDE * DEPTH * WIDTH, 5 << 20),
        name="range_part",
    )(notes, here, msg, weights)


def turn_kernel(msg_ref, out_ref):
    for s in range(NX):
        high, low = split(msg_ref[0, pl.ds(s * SIDE, SIDE)].T)
        out_ref[0, s, :, pl.ds(0, SIDE)] = high
        out_ref[0, s, :, pl.ds(SIDE, SIDE)] = low


def turn(msg):
    return pl.pallas_call(
        turn_kernel,
        grid=(8,),
        out_shape=jax.ShapeDtypeStruct((8, NX, SIDE, 2 * SIDE), BF16),
        in_specs=[pl.BlockSpec((1, ROWS, SIDE), lambda d: (d, 0, 0))],
        out_specs=pl.BlockSpec((1, NX, SIDE, 2 * SIDE), lambda d: (d, 0, 0, 0)),
        compiler_params=params(),
        cost_estimate=cost(1 << 20, 4 << 20),
        name="turn",
    )(msg)


def corange_kernel(n0_ref, n1_ref, here_ref, t0_ref, t1_ref, *refs):
    near_refs, (out_ref, stack_ref) = refs[:NX], refs[NX:]
    step = pl.program_id(0)
    d = step % 4 * 2 + (here_ref[1] + step // 4) % 2

    @pl.when(step == 0)
    def _():
        for s, ref in enumerate(near_refs):
            for k in range(4):
                high, low = split(ref[k])
                stack_ref[s * 4 + k, pl.ds(0, SIDE)] = high
                stack_ref[s * 4 + k, pl.ds(SIDE, SIDE)] = high
                stack_ref[s * 4 + k, pl.ds(2 * SIDE, SIDE)] = low

    @pl.when(step % 4 == 0)
    def _():
        out_ref[...] = jnp.zeros_like(out_ref)

    for h, (n_ref, t_ref) in enumerate(((n0_ref, t0_ref), (n1_ref, t1_ref))):
        for s in range(NX):
            note = n_ref[d * NX + s]
            place = jnp.maximum(note, 0)
            pair = jnp.where(note >= 0, t_ref[0, s], jnp.zeros((), BF16))
            left = jnp.concatenate([pair, pair[:, :SIDE]], axis=1)
            right = stack_ref[s * 4 + h * 2 + place // CT_DEV]
            out_ref[0, place % CT_DEV] += jnp.dot(left, right, preferred_element_type=F32)


def corange_part(notes, here, turned, near):
    def of_source(step, n0, n1, here):
        return (step % 4 * 2 + (here[1] + step // 4) % 2, 0, 0, 0)

    return pl.pallas_call(
        corange_kernel,
        out_shape=jax.ShapeDtypeStruct((2, CT_DEV, SIDE, WIDTH), F32),
        grid_spec=pltpu.PrefetchScalarGridSpec(
            num_scalar_prefetch=3,
            grid=(8,),
            in_specs=[pl.BlockSpec((1, NX, SIDE, 2 * SIDE), of_source)] * 2
            + [pl.BlockSpec((4, SIDE, WIDTH), lambda d, *_: (0, 0, 0))] * NX,
            out_specs=pl.BlockSpec((1, CT_DEV, SIDE, WIDTH), lambda step, *_: (step // 4, 0, 0, 0)),
            scratch_shapes=[pltpu.VMEM((16, DEPTH, WIDTH), BF16)],
        ),
        compiler_params=params(),
        cost_estimate=cost(64 * 2 * SIDE * DEPTH * WIDTH, 8 << 20),
        name="corange_part",
    )(*notes, here, *turned, *near)


def exchange(value, axes):
    return lax.all_to_all(value, axes, split_axis=0, concat_axis=0, tiled=True)


def shifted(value, axis, step):
    n = lax.axis_size(axis)
    return lax.ppermute(value, axis, [(i, (i + step) % n) for i in range(n)])


def on_device(tiles, tile_dest, tile_row, tile_col, omega, col_scale):
    y, z, x = lax.axis_index("y"), lax.axis_index("z"), lax.axis_index("x")
    here = jnp.stack([y, lax.axis_index("c")]).astype(jnp.int32)
    weights = col_scale.astype(F32)

    packed = pack(
        tile_dest[0, 0, :, 0], tile_row[0, 0], tile_col[0, 0], x.reshape(1), tiles[0, 0]
    )
    scaled = (omega * weights[:, None]).reshape(CT_DEV, SIDE, WIDTH)
    stacked = stack(scaled, shifted(scaled, "c", 1))

    notes, turned, parts = [], [], []
    for h in range(2):
        msg = exchange(packed[h], ("y", "c"))
        note = msg[:, NX * SIDE, :NX].reshape(8 * NX).astype(jnp.int32)
        blocks = range_part(note, here, msg, stacked)
        part = blocks[0]
        for s in range(1, NX):
            part = part + shifted(blocks[s], "x", s)
        notes.append(note)
        turned.append(turn(msg))
        parts.append(part)
    part = jnp.concatenate(parts).reshape(8, 64, WIDTH)
    part = exchange(part, "z").sum(axis=0)
    near = exchange(jnp.broadcast_to(part[None], (8, 64, WIDTH)), "z").reshape(4, SIDE, WIDTH)

    mine = lax.dynamic_slice_in_dim(near, z // 4 * 2, 2, axis=0).reshape(2 * SIDE, WIDTH)
    range_local = jnp.where(z % 4 == y, mine, 0.0)
    for step in range(1, 4):
        pairs = []
        for i in range(64):
            start = i // 8 % 4
            pairs.append((start * 64 + i, (start + step) % 4 * 64 + i))
        range_local = range_local + lax.ppermute(mine, ("y", "z", "x", "c"), pairs)

    around = [near] + [shifted(near, "x", -s) for s in range(1, NX)]
    own, other = corange_part(notes, here, turned, around)
    total = own + shifted(other, "c", 1)
    columns = total[0]
    for s in range(1, 4):
        columns = columns + shifted(total[s], "y", s)
    columns = columns * lax.dynamic_slice_in_dim(weights, y * SIDE, SIDE, axis=0)[:, None]
    columns = jnp.stack([columns] + [shifted(columns, "y", s) for s in range(1, 4)])
    order = (y - jnp.arange(4, dtype=jnp.int32)) % 4
    corange_local = jnp.take(columns, order, axis=0).reshape(CT_DEV * SIDE, WIDTH)
    return range_local, corange_local


def solution(mesh):
    fine = Mesh(mesh.devices.reshape(4, 8, 4, 2), ("y", "z", "x", "c"))
    lane = ("z", "x", "c")
    placed = (
        P("y", lane, None, None, None),
        P("y", lane, None, None),
        P("y", lane, None),
        P("y", lane, None),
        P(lane, None),
        P(lane),
    )
    return jax.shard_map(
        on_device,
        mesh=fine,
        in_specs=placed,
        out_specs=(P(lane, None), P(lane, None)),
        check_vma=False,
    )
```

```python
import functools

import jax
import jax.numpy as jnp
from jax import lax
from jax.experimental import pallas as pl
from jax.experimental.pallas import tpu as pltpu
from jax.sharding import Mesh, PartitionSpec as P

SIDE = 128
WIDTH = 256
CT_DEV = 4
NX = 4
HALF = SIDE // 2
FIRST = NX * (SIDE + HALF) + 8
SECOND = NX * HALF
DEPTH = 3 * SIDE
VMEM = 20 * 1024 * 1024
F32 = jnp.float32
BF16 = jnp.bfloat16


def split(value):
    high = value.astype(BF16)
    low = (value - high.astype(F32)).astype(BF16)
    return high, low


def params():
    return pltpu.CompilerParams(vmem_limit_bytes=VMEM)


def cost(flops, size):
    return pl.CostEstimate(flops=flops, bytes_accessed=size, transcendentals=0)


def pack_kernel(x_ref, dest_ref, row_ref, col_ref, tiles_ref, first_ref, second_ref, *scratch):
    from_ref, note_ref, *held = scratch[:5]
    sems = scratch[5]
    d = pl.program_id(0)

    @pl.when(d == 0)
    def _():
        copies = [
            pltpu.make_async_copy(source, target, sems.at[i])
            for i, (source, target) in enumerate(zip((dest_ref, row_ref, col_ref), held))
        ]
        for copy in copies:
            copy.start()
        for i in range(64):
            from_ref[i] = 0
            note_ref[i] = -1
        for copy in copies:
            copy.wait()

        @pl.loop(0, tiles_ref.shape[0])
        def _(t):
            lane = held[0][t]
            z, x, c = lane // 8, lane // 2 % 4, lane % 2
            to = z % 4
            slot = (to * 2 + c) * 8 + z // 4 * 4 + (x - x_ref[0] + 4) % 4
            from_ref[slot] = t
            note_ref[slot] = held[1][t] * CT_DEV + (held[2][t] - to + 4) % 4

    spot = lax.broadcasted_iota(jnp.int32, (8, SIDE), 1)
    notes = jnp.full((8, SIDE), -1, jnp.int32)
    for k in range(2 * NX):
        slot = d * 8 + k
        t = from_ref[slot]
        notes = jnp.where(spot == k, note_ref[slot], notes)
        if k < NX:
            first_ref[0, pl.ds(k * SIDE, SIDE)] = tiles_ref[t]
        else:
            s = k - NX
            first_ref[0, pl.ds(NX * SIDE + s * HALF, HALF)] = tiles_ref[t, pl.ds(0, HALF)]
            second_ref[0, pl.ds(s * HALF, HALF)] = tiles_ref[t, pl.ds(HALF, HALF)]
    first_ref[0, pl.ds(FIRST - 8, 8)] = notes.astype(F32)


def pack(x, dest, row, col, tiles):
    hbm = pl.BlockSpec(memory_space=pl.ANY)
    return pl.pallas_call(
        pack_kernel,
        grid=(8,),
        out_shape=[
            jax.ShapeDtypeStruct((8, FIRST, SIDE), F32),
            jax.ShapeDtypeStruct((8, SECOND, SIDE), F32),
        ],
        in_specs=[pl.BlockSpec(memory_space=pltpu.SMEM)]
        + [hbm] * 3
        + [pl.BlockSpec(tiles.shape, lambda d: (0, 0, 0))],
        out_specs=[
            pl.BlockSpec((1, FIRST, SIDE), lambda d: (d, 0, 0)),
            pl.BlockSpec((1, SECOND, SIDE), lambda d: (d, 0, 0)),
        ],
        scratch_shapes=[pltpu.SMEM((64,), jnp.int32)] * 2
        + [pltpu.SMEM(dest.shape, jnp.int32)] * 3
        + [pltpu.SemaphoreType.DMA((3,))],
        compiler_params=params(),
        name="pack",
    )(x, dest, row, col, tiles)


def stack_kernel(own_ref, other_ref, out_ref):
    for i, ref in enumerate((own_ref, other_ref)):
        for k in range(CT_DEV):
            high, low = split(ref[k])
            out_ref[i * CT_DEV + k, pl.ds(0, SIDE)] = high
            out_ref[i * CT_DEV + k, pl.ds(SIDE, SIDE)] = high
            out_ref[i * CT_DEV + k, pl.ds(2 * SIDE, SIDE)] = low


def stack(own, other):
    return pl.pallas_call(
        stack_kernel,
        out_shape=jax.ShapeDtypeStruct((2 * CT_DEV, DEPTH, WIDTH), BF16),
        compiler_params=params(),
        cost_estimate=cost(1 << 20, 3 << 20),
        name="stack",
    )(own, other)


def range_kernel(pieces, note_ref, here_ref, msg_ref, stack_ref, *out_refs):
    d = pl.program_id(0)

    @pl.when(d == 0)
    def _():
        for ref in out_refs:
            ref[...] = jnp.zeros_like(ref)

    base = jnp.where(lax.rem(d, 2) == here_ref[1], 0, CT_DEV)
    for h, start, rows, out in pieces:
        for s, ref in enumerate(out_refs):
            note = note_ref[d * 2 * NX + h * NX + s]
            place = jnp.maximum(note, 0)
            col = base + (place + here_ref[0]) % CT_DEV
            tile = jnp.where(note >= 0, msg_ref[0, pl.ds(start + s * rows, rows)], 0.0)
            high, low = split(tile)
            left = jnp.concatenate([high, low, high], axis=1)
            spot = pl.ds(pl.multiple_of(out + place // CT_DEV * rows, HALF), rows)
            ref[spot] += jnp.dot(left, stack_ref[col], preferred_element_type=F32)


def range_part(pieces, notes, here, msg, weights):
    rows = 2 * sum(piece[2] for piece in pieces)
    return pl.pallas_call(
        functools.partial(range_kernel, pieces),
        out_shape=[jax.ShapeDtypeStruct((rows, WIDTH), F32)] * NX,
        grid_spec=pltpu.PrefetchScalarGridSpec(
            num_scalar_prefetch=2,
            grid=(8,),
            in_specs=[
                pl.BlockSpec((1,) + msg.shape[1:], lambda d, *_: (d, 0, 0)),
                pl.BlockSpec(weights.shape, lambda d, *_: (0, 0, 0)),
            ],
            out_specs=[pl.BlockSpec((rows, WIDTH), lambda d, *_: (0, 0))] * NX,
        ),
        compiler_params=params(),
        cost_estimate=cost(16 * rows * 2 * DEPTH * WIDTH, 5 << 20),
        name="range_part",
    )(notes, here, msg, weights)


def turn_kernel(first_ref, second_ref, *out_refs):
    for s, ref in enumerate(out_refs):
        whole = first_ref[0, pl.ds(s * SIDE, SIDE)]
        halves = jnp.concatenate(
            [first_ref[0, pl.ds(NX * SIDE + s * HALF, HALF)], second_ref[0, pl.ds(s * HALF, HALF)]]
        )
        for h, tile in enumerate((whole, halves)):
            high, low = split(tile.T)
            ref[0, h, :, pl.ds(0, SIDE)] = high
            ref[0, h, :, pl.ds(SIDE, SIDE)] = low


def turn(first, second):
    return pl.pallas_call(
        turn_kernel,
        grid=(8,),
        out_shape=[jax.ShapeDtypeStruct((8, 2, SIDE, 2 * SIDE), BF16)] * NX,
        in_specs=[
            pl.BlockSpec((1, FIRST, SIDE), lambda d: (d, 0, 0)),
            pl.BlockSpec((1, SECOND, SIDE), lambda d: (d, 0, 0)),
        ],
        out_specs=[pl.BlockSpec((1, 2, SIDE, 2 * SIDE), lambda d: (d, 0, 0, 0))] * NX,
        compiler_params=params(),
        cost_estimate=cost(1 << 20, 8 << 20),
        name="turn",
    )(first, second)


def corange_kernel(steps, resumed, note_ref, here_ref, *refs):
    count = len(steps)
    turned_refs, near_refs, refs = refs[:count], refs[count : 2 * count], refs[2 * count :]
    if resumed:
        before, refs = refs[:2], refs[2:]
    *out_refs, stack_ref = refs
    step = pl.program_id(0)
    which = step // 4
    d = step % 4 * 2 + (here_ref[1] + which) % 2

    @pl.when(step == 0)
    def _():
        for i, ref in enumerate(near_refs):
            for k in range(4):
                if k < 2:
                    rows = ref[pl.ds(k * SIDE, SIDE)]
                else:
                    r = k - 2
                    rows = jnp.concatenate(
                        [ref[pl.ds(256 + r * HALF, HALF)], ref[pl.ds(384 + r * HALF, HALF)]]
                    )
                high, low = split(rows)
                stack_ref[i * 4 + k, pl.ds(0, SIDE)] = high
                stack_ref[i * 4 + k, pl.ds(SIDE, SIDE)] = high
                stack_ref[i * 4 + k, pl.ds(2 * SIDE, SIDE)] = low
        for i, ref in enumerate(out_refs):
            ref[...] = before[i][...] if resumed else jnp.zeros_like(ref)

    for w, out_ref in enumerate(out_refs):

        @pl.when(which == w)
        def _():
            for i, s in enumerate(steps):
                for h in range(2):
                    note = note_ref[d * 2 * NX + h * NX + s]
                    place = jnp.maximum(note, 0)
                    pair = jnp.where(note >= 0, turned_refs[i][0, h], jnp.zeros((), BF16))
                    left = jnp.concatenate([pair, pair[:, :SIDE]], axis=1)
                    right = stack_ref[i * 4 + h * 2 + place // CT_DEV]
                    out_ref[place % CT_DEV] += jnp.dot(left, right, preferred_element_type=F32)


def corange_part(steps, notes, here, turned, near, before=()):
    def of_source(step, notes, here):
        return (step % 4 * 2 + (here[1] + step // 4) % 2, 0, 0, 0)

    whole = pl.BlockSpec((CT_DEV, SIDE, WIDTH), lambda d, *_: (0, 0, 0))
    count = len(steps)
    return pl.pallas_call(
        functools.partial(corange_kernel, steps, bool(before)),
        out_shape=[jax.ShapeDtypeStruct((CT_DEV, SIDE, WIDTH), F32)] * 2,
        grid_spec=pltpu.PrefetchScalarGridSpec(
            num_scalar_prefetch=2,
            grid=(8,),
            in_specs=[pl.BlockSpec((1, 2, SIDE, 2 * SIDE), of_source)] * count
            + [pl.BlockSpec((4 * SIDE, WIDTH), lambda d, *_: (0, 0))] * count
            + [whole] * len(before),
            out_specs=[whole] * 2,
            scratch_shapes=[pltpu.VMEM((4 * count, DEPTH, WIDTH), BF16)],
        ),
        compiler_params=params(),
        cost_estimate=cost(count * 16 * 2 * SIDE * DEPTH * WIDTH, count << 21),
        name="corange_part",
    )(notes, here, *turned, *near, *before)


def join_kernel(a_ref, b_ref, *out_refs):
    for k, ref in enumerate(out_refs):
        ref[...] = a_ref[k] + b_ref[k]


def join(a, b):
    return pl.pallas_call(
        join_kernel,
        out_shape=[jax.ShapeDtypeStruct((SIDE, WIDTH), F32)] * CT_DEV,
        compiler_params=params(),
        name="join",
    )(a, b)


def place_kernel(here_ref, *refs):
    *in_refs, out_ref = refs
    for s, ref in enumerate(in_refs):
        spot = (here_ref[0] - s + 4) % 4
        out_ref[pl.ds(pl.multiple_of(spot * SIDE, SIDE), SIDE)] = ref[...]


def place(here, *columns):
    vmem = pl.BlockSpec(memory_space=pltpu.VMEM)
    return pl.pallas_call(
        place_kernel,
        out_shape=jax.ShapeDtypeStruct((CT_DEV * SIDE, WIDTH), F32),
        in_specs=[pl.BlockSpec(memory_space=pltpu.SMEM)] + [vmem] * 4,
        out_specs=vmem,
        compiler_params=params(),
        name="place",
    )(here, *columns)


def exchange(value, axes):
    return lax.all_to_all(value, axes, split_axis=0, concat_axis=0, tiled=True)


def shifted(value, axis, step):
    n = lax.axis_size(axis)
    return lax.ppermute(value, axis, [(i, (i + step) % n) for i in range(n)])


def on_device(tiles, tile_dest, tile_row, tile_col, omega, col_scale):
    y, z, x = (lax.axis_index(name) for name in "yzx")
    here = jnp.stack([y, lax.axis_index("c")]).astype(jnp.int32)
    weights = col_scale.astype(F32)

    first, second = pack(
        x.reshape(1), tile_dest[0, 0, :, 0], tile_row[0, 0], tile_col[0, 0], tiles[0, 0]
    )
    scaled = (omega * weights[:, None]).reshape(CT_DEV, SIDE, WIDTH)
    stacked = stack(scaled, shifted(scaled, "c", 1))

    first = exchange(first, ("y", "c"))
    notes = first[:, FIRST - 8, : 2 * NX].reshape(16 * NX).astype(jnp.int32)
    second = exchange(second, ("y", "c"))
    parts = []
    for msg, pieces in (
        (first, ((0, 0, SIDE, 0), (1, NX * SIDE, HALF, 2 * SIDE))),
        (second, ((1, 0, HALF, 0),)),
    ):
        blocks = range_part(pieces, notes, here, msg, stacked)
        part = blocks[0]
        for s in range(1, NX):
            part = part + shifted(blocks[s], "x", s)
        parts.append(part)
    turned = turn(first, second)
    part = jnp.concatenate(parts).reshape(8, 64, WIDTH)
    part = exchange(part, "z").sum(axis=0)
    near = exchange(jnp.broadcast_to(part[None], (8, 64, WIDTH)), "z").reshape(4 * SIDE, WIDTH)

    later = [near[i : i + HALF] for i in (2 * SIDE, 3 * SIDE, 2 * SIDE + HALF, 3 * SIDE + HALF)]
    mine = jnp.where(z >= 4, jnp.concatenate(later), near[: 2 * SIDE])
    range_local = jnp.where(z % 4 == y, mine, 0.0)
    for step in range(1, 4):
        pairs = []
        for i in range(64):
            start = i // 8 % 4
            pairs.append((start * 64 + i, (start + step) % 4 * 64 + i))
        range_local = range_local + lax.ppermute(mine, ("y", "z", "x", "c"), pairs)

    around = [near] + [shifted(near, "x", -s) for s in range(1, NX)]
    early, late = (0, 1, 3), (2,)
    pick = lambda arrays, steps: [arrays[s] for s in steps]
    so_far = corange_part(early, notes, here, pick(turned, early), pick(around, early))
    around[2], range_local = lax.optimization_barrier((around[2], range_local))
    own, other = corange_part(late, notes, here, pick(turned, late), pick(around, late), so_far)
    total = join(own, shifted(other, "c", 1))
    columns = total[0]
    for s in range(1, 4):
        columns = columns + shifted(total[s], "y", s)
    columns = columns * lax.dynamic_slice_in_dim(weights, y * SIDE, SIDE, axis=0)[:, None]
    corange_local = place(here, columns, *[shifted(columns, "y", s) for s in range(1, 4)])
    return range_local, corange_local


def solution(mesh):
    fine = Mesh(mesh.devices.reshape(4, 8, 4, 2), ("y", "z", "x", "c"))
    lane = ("z", "x", "c")
    placed = (
        P("y", lane, None, None, None),
        P("y", lane, None, None),
        P("y", lane, None),
        P("y", lane, None),
        P(lane, None),
        P(lane),
    )
    return jax.shard_map(
        on_device,
        mesh=fine,
        in_specs=placed,
        out_specs=(P(lane, None), P(lane, None)),
        check_vma=False,
    )
```

```python
import functools

import jax
import jax.numpy as jnp
from jax import lax
from jax.experimental import pallas as pl
from jax.experimental.pallas import tpu as pltpu
from jax.sharding import Mesh, PartitionSpec as P

SIDE = 128
WIDTH = 256
CT_DEV = 4
NX = 4
HALF = SIDE // 2
FIRST = NX * (SIDE + HALF) + 8
SECOND = NX * HALF
DEPTH = 3 * SIDE
VMEM = 12 * 1024 * 1024
F32 = jnp.float32
BF16 = jnp.bfloat16


def split(value):
    high = value.astype(BF16)
    low = (value - high.astype(F32)).astype(BF16)
    return high, low


def params():
    return pltpu.CompilerParams(vmem_limit_bytes=VMEM)


def cost(flops, size):
    return pl.CostEstimate(flops=flops, bytes_accessed=size, transcendentals=0)


def pack_kernel(x_ref, index_ref, tiles_ref, first_ref, second_ref, from_ref, note_ref):
    d = pl.program_id(0)

    @pl.when(d == 0)
    def _():
        for i in range(64):
            from_ref[i] = 0
            note_ref[i] = -1

        @pl.loop(0, tiles_ref.shape[0])
        def _(t):
            index = index_ref[t]
            lane = index // 8
            z, x, c = lane // 8, lane // 2 % 4, lane % 2
            to = z % 4
            slot = (to * 2 + c) * 8 + z // 4 * 4 + (x - x_ref[0] + 4) % 4
            from_ref[slot] = t
            note_ref[slot] = index // 4 % 2 * CT_DEV + (index - to + 64) % 4

    spot = lax.broadcasted_iota(jnp.int32, (8, SIDE), 1)
    notes = jnp.full((8, SIDE), -1, jnp.int32)
    for k in range(2 * NX):
        slot = d * 8 + k
        t = from_ref[slot]
        notes = jnp.where(spot == k, note_ref[slot], notes)
        if k < NX:
            first_ref[0, pl.ds(k * SIDE, SIDE)] = tiles_ref[t]
        else:
            s = k - NX
            first_ref[0, pl.ds(NX * SIDE + s * HALF, HALF)] = tiles_ref[t, pl.ds(0, HALF)]
            second_ref[0, pl.ds(s * HALF, HALF)] = tiles_ref[t, pl.ds(HALF, HALF)]
    first_ref[0, pl.ds(FIRST - 8, 8)] = notes.astype(F32)


def pack(x, index, tiles):
    return pl.pallas_call(
        pack_kernel,
        grid=(8,),
        out_shape=[
            jax.ShapeDtypeStruct((8, FIRST, SIDE), F32),
            jax.ShapeDtypeStruct((8, SECOND, SIDE), F32),
        ],
        in_specs=[pl.BlockSpec(memory_space=pltpu.SMEM)] * 2
        + [pl.BlockSpec(tiles.shape, lambda d: (0, 0, 0))],
        out_specs=[
            pl.BlockSpec((1, FIRST, SIDE), lambda d: (d, 0, 0)),
            pl.BlockSpec((1, SECOND, SIDE), lambda d: (d, 0, 0)),
        ],
        scratch_shapes=[pltpu.SMEM((64,), jnp.int32)] * 2,
        compiler_params=params(),
        name="pack",
    )(x, index, tiles)


def stack_kernel(own_ref, other_ref, out_ref):
    for i, ref in enumerate((own_ref, other_ref)):
        for k in range(CT_DEV):
            high, low = split(ref[k])
            out_ref[i * CT_DEV + k, pl.ds(0, SIDE)] = high
            out_ref[i * CT_DEV + k, pl.ds(SIDE, SIDE)] = high
            out_ref[i * CT_DEV + k, pl.ds(2 * SIDE, SIDE)] = low


def stack(own, other):
    return pl.pallas_call(
        stack_kernel,
        out_shape=jax.ShapeDtypeStruct((2 * CT_DEV, DEPTH, WIDTH), BF16),
        compiler_params=params(),
        cost_estimate=cost(1 << 20, 3 << 20),
        name="stack",
    )(own, other)


def range_kernel(pieces, note_ref, here_ref, msg_ref, stack_ref, *out_refs):
    for ref in out_refs:
        ref[...] = jnp.zeros_like(ref)

    @pl.loop(0, 8)
    def _(d):
        base = jnp.where(lax.rem(d, 2) == here_ref[1], 0, CT_DEV)
        for h, start, rows, out in pieces:
            for s, ref in enumerate(out_refs):
                note = note_ref[d * 2 * NX + h * NX + s]
                place = jnp.maximum(note, 0)
                col = base + (place + here_ref[0]) % CT_DEV
                tile = jnp.where(note >= 0, msg_ref[d, pl.ds(start + s * rows, rows)], 0.0)
                high, low = split(tile)
                left = jnp.concatenate([high, low, high], axis=1)
                spot = pl.ds(pl.multiple_of(out + place // CT_DEV * rows, HALF), rows)
                ref[spot] += jnp.dot(left, stack_ref[col], preferred_element_type=F32)


def on_chip(kernel, name, scalars, arrays, out_shape, scratch=(), flops=1 << 20, size=1 << 20):
    many = isinstance(out_shape, list)
    vmem, smem = (pl.BlockSpec(memory_space=space) for space in (pltpu.VMEM, pltpu.SMEM))
    return pl.pallas_call(
        kernel,
        out_shape=out_shape,
        in_specs=[smem] * len(scalars) + [vmem] * len(arrays),
        out_specs=[vmem] * len(out_shape) if many else vmem,
        scratch_shapes=list(scratch),
        compiler_params=params(),
        cost_estimate=cost(flops, size),
        name=name,
    )(*scalars, *arrays)


def range_part(pieces, notes, here, msg, weights):
    rows = 2 * sum(piece[2] for piece in pieces)
    shape = [jax.ShapeDtypeStruct((rows, WIDTH), F32)] * NX
    kernel = functools.partial(range_kernel, pieces)
    return on_chip(kernel, "range_part", (notes, here), (msg, weights), shape, size=1 << 22)


def turn_kernel(first_ref, second_ref, *out_refs):
    @pl.loop(0, 8)
    def _(d):
        for s, ref in enumerate(out_refs):
            whole = first_ref[d, pl.ds(s * SIDE, SIDE)]
            start = NX * SIDE + s * HALF
            halves = [first_ref[d, pl.ds(start, HALF)], second_ref[d, pl.ds(s * HALF, HALF)]]
            for h, tile in enumerate((whole, jnp.concatenate(halves))):
                high, low = split(tile.T)
                ref[d, h, :, pl.ds(0, SIDE)] = high
                ref[d, h, :, pl.ds(SIDE, SIDE)] = low


def turn(first, second):
    shape = [jax.ShapeDtypeStruct((8, 2, SIDE, 2 * SIDE), BF16)] * NX
    return on_chip(turn_kernel, "turn", (), (first, second), shape, size=8 << 20)


def corange_kernel(note_ref, here_ref, *refs):
    turned_refs, near_refs, (*out_refs, stack_ref) = refs[:NX], refs[NX : 2 * NX], refs[2 * NX :]

    for s, ref in enumerate(near_refs):
        for k in range(4):
            high, low = split(ref[pl.ds(k * SIDE, SIDE)])
            stack_ref[s * 4 + k, pl.ds(0, SIDE)] = high
            stack_ref[s * 4 + k, pl.ds(SIDE, SIDE)] = high
            stack_ref[s * 4 + k, pl.ds(2 * SIDE, SIDE)] = low

    for which, out_ref in enumerate(out_refs):
        out_ref[...] = jnp.zeros_like(out_ref)

        @pl.loop(0, 4)
        def _(source):
            d = source * 2 + (here_ref[1] + which) % 2
            for s in range(NX):
                for h in range(2):
                    note = note_ref[d * 2 * NX + h * NX + s]
                    place = jnp.maximum(note, 0)
                    pair = jnp.where(note >= 0, turned_refs[s][d, h], jnp.zeros((), BF16))
                    left = jnp.concatenate([pair, pair[:, :SIDE]], axis=1)
                    right = stack_ref[s * 4 + h * 2 + place // CT_DEV]
                    out_ref[place % CT_DEV] += jnp.dot(left, right, preferred_element_type=F32)


def corange_part(notes, here, turned, near):
    shape = [jax.ShapeDtypeStruct((CT_DEV, SIDE, WIDTH), F32)] * 2
    scratch = [pltpu.VMEM((4 * NX, DEPTH, WIDTH), BF16)]
    arrays = (*turned, *near)
    return on_chip(corange_kernel, "corange_part", (notes, here), arrays, shape, scratch)


def gather_sum_kernel(in_ref, out_ref):
    total = in_ref[0]
    for k in range(1, 8):
        total = total + in_ref[k]
    for k in range(8):
        out_ref[k] = total


def gather_sum(parts):
    shape = jax.ShapeDtypeStruct(parts.shape, F32)
    return on_chip(gather_sum_kernel, "gather_sum", (), (parts,), shape)


def join_kernel(a_ref, b_ref, *out_refs):
    for k, ref in enumerate(out_refs):
        ref[...] = a_ref[k] + b_ref[k]


def join(a, b):
    shape = [jax.ShapeDtypeStruct((SIDE, WIDTH), F32)] * CT_DEV
    return on_chip(join_kernel, "join", (), (a, b), shape)


def place_kernel(here_ref, *refs):
    *in_refs, out_ref = refs
    for s, ref in enumerate(in_refs):
        spot = (here_ref[0] - s + 4) % 4
        out_ref[pl.ds(pl.multiple_of(spot * SIDE, SIDE), SIDE)] = ref[...]


def place(here, *columns):
    shape = jax.ShapeDtypeStruct((CT_DEV * SIDE, WIDTH), F32)
    return on_chip(place_kernel, "place", (here,), columns, shape)


def exchange(value, axes):
    return lax.all_to_all(value, axes, split_axis=0, concat_axis=0, tiled=True)


def shifted(value, axis, step):
    n = lax.axis_size(axis)
    return lax.ppermute(value, axis, [(i, (i + step) % n) for i in range(n)])


def on_device(tiles, tile_dest, tile_row, tile_col, omega, col_scale):
    y, z, x = (lax.axis_index(name) for name in "yzx")
    here = jnp.stack([y, lax.axis_index("c")]).astype(jnp.int32)
    weights = col_scale.astype(F32)

    index = tile_dest[0, 0, :, 0] * 8 + tile_row[0, 0] * 4 + tile_col[0, 0]
    first, second = pack(x.reshape(1), index, tiles[0, 0])
    scaled = (omega * weights[:, None]).reshape(CT_DEV, SIDE, WIDTH)
    stacked = stack(scaled, shifted(scaled, "c", 1))

    first = exchange(first, ("y", "c"))
    notes = first[:, FIRST - 8, : 2 * NX].reshape(16 * NX).astype(jnp.int32)
    second, stacked = lax.optimization_barrier((second, stacked))
    second = exchange(second, ("y", "c"))
    parts = []
    for msg, pieces in (
        (first, ((0, 0, SIDE, 0), (1, NX * SIDE, HALF, 2 * SIDE))),
        (second, ((1, 0, HALF, 0),)),
    ):
        blocks = range_part(pieces, notes, here, msg, stacked)
        if parts:
            *blocks, parts[0] = lax.optimization_barrier((*blocks, parts[0]))
        part = blocks[0]
        for s in range(1, NX):
            part = part + shifted(blocks[s], "x", s)
        parts.append(part)
    turned = turn(first, second)
    a, b = parts
    part = jnp.concatenate([a[: 2 * SIDE], a[256:320], b[:HALF], a[320:], b[HALF:]])
    part = gather_sum(exchange(part.reshape(8, 64, WIDTH), "z"))
    near = exchange(part, "z").reshape(4 * SIDE, WIDTH)

    mine = lax.dynamic_slice_in_dim(near, z // 4 * 2 * SIDE, 2 * SIDE, axis=0)
    range_local = jnp.where(z % 4 == y, mine, 0.0)
    for step in range(1, 4):
        pairs = []
        for i in range(64):
            start = i // 8 % 4
            pairs.append((start * 64 + i, (start + step) % 4 * 64 + i))
        range_local = range_local + lax.ppermute(mine, ("y", "z", "x", "c"), pairs)

    around = [near] + [shifted(near, "x", -s) for s in range(1, NX)]
    around[2], range_local = lax.optimization_barrier((around[2], range_local))
    own, other = corange_part(notes, here, turned, around)
    total = join(own, shifted(other, "c", 1))
    columns = total[0]
    for s in range(1, 4):
        columns = columns + shifted(total[s], "y", s)
    columns = columns * lax.dynamic_slice_in_dim(weights, y * SIDE, SIDE, axis=0)[:, None]
    corange_local = place(here, columns, *[shifted(columns, "y", s) for s in range(1, 4)])
    return range_local, corange_local


def solution(mesh):
    fine = Mesh(mesh.devices.reshape(4, 8, 4, 2), ("y", "z", "x", "c"))
    lane = ("z", "x", "c")
    placed = (
        P("y", lane, None, None, None),
        P("y", lane, None, None),
        P("y", lane, None),
        P("y", lane, None),
        P(lane, None),
        P(lane),
    )
    return jax.shard_map(
        on_device,
        mesh=fine,
        in_specs=placed,
        out_specs=(P(lane, None), P(lane, None)),
        check_vma=False,
    )
```

```python
import functools

import jax
import jax.numpy as jnp
from jax import lax
from jax.experimental import pallas as pl
from jax.experimental.pallas import tpu as pltpu
from jax.sharding import Mesh, PartitionSpec as P

SIDE = 128
WIDTH = 256
CT_DEV = 4
NX = 4
DEPTH = 3 * SIDE
PART = SIDE // 4
HALF = SIDE // 2
SPLIT = 4
VMEM = 12 * 1024 * 1024
F32 = jnp.float32
BF16 = jnp.bfloat16


def split(value):
    high = value.astype(BF16)
    low = (value - high.astype(F32)).astype(BF16)
    return high, low


def params():
    return pltpu.CompilerParams(vmem_limit_bytes=VMEM)


def cost(flops, size):
    return pl.CostEstimate(flops=flops, bytes_accessed=size, transcendentals=0)


def on_chip(kernel, name, scalars, arrays, out_shape, scratch=(), flops=1 << 20, size=1 << 20):
    many = isinstance(out_shape, list)
    vmem, smem = (pl.BlockSpec(memory_space=space) for space in (pltpu.VMEM, pltpu.SMEM))
    return pl.pallas_call(
        kernel,
        out_shape=out_shape,
        in_specs=[smem] * len(scalars) + [vmem] * len(arrays),
        out_specs=[vmem] * len(out_shape) if many else vmem,
        scratch_shapes=list(scratch),
        compiler_params=params(),
        cost_estimate=cost(flops, size),
        name=name,
    )(*scalars, *arrays)


def source(here_ref, k):
    return (here_ref[0] - k // 2 + 4) % 4 * 2 + (here_ref[1] + k) % 2


def pack_kernel(here_ref, index_ref, tiles_ref, *refs):
    out_refs, (from_ref, note_ref) = refs[:-2], refs[-2:]
    for i in range(64):
        from_ref[i] = 0
        note_ref[i] = -1

    @pl.loop(0, tiles_ref.shape[0])
    def _(t):
        index = index_ref[t]
        lane = index // 8
        z, x, c = lane // 8, lane // 2 % 4, lane % 2
        k = (x - here_ref[0] + 4) % 4 * 2 + (c + here_ref[1]) % 2
        slot = k * 8 + z
        from_ref[slot] = t
        note_ref[slot] = index // 4 % 2 * CT_DEV + (index - x + 64) % 4

    spot = lax.broadcasted_iota(jnp.int32, (8, SIDE), 1)
    for k in range(8):
        first_ref = out_refs[8].at[(here_ref[0] + k // 2) % 4 * 2 + (here_ref[1] + k) % 2]
        notes = jnp.full((8, SIDE), -1, jnp.int32)
        for z in range(8):
            slot = k * 8 + z
            notes = jnp.where(spot == z, note_ref[slot], notes)
            ref = out_refs[k] if z >= SPLIT else first_ref
            ref[pl.ds(z % SPLIT * SIDE, SIDE)] = tiles_ref[from_ref[slot]]
        first_ref[pl.ds(SPLIT * SIDE, 8)] = notes.astype(F32)


def pack(here, index, tiles):
    shape = [jax.ShapeDtypeStruct(((8 - SPLIT) * SIDE, SIDE), F32)] * 8
    shape += [jax.ShapeDtypeStruct((8, SPLIT * SIDE + 8, SIDE), F32)]
    scratch = [pltpu.SMEM((64,), jnp.int32)] * 2
    out = on_chip(pack_kernel, "pack", (here, index), (tiles,), shape, scratch, size=8 << 20)
    return out[8], list(out[:8])


def stack_kernel(own_ref, other_ref, out_ref):
    for i, ref in enumerate((own_ref, other_ref)):
        for k in range(CT_DEV):
            high, low = split(ref[k])
            out_ref[i * CT_DEV + k, pl.ds(0, SIDE)] = high
            out_ref[i * CT_DEV + k, pl.ds(SIDE, SIDE)] = high
            out_ref[i * CT_DEV + k, pl.ds(2 * SIDE, SIDE)] = low


def stack(own, other):
    return pl.pallas_call(
        stack_kernel,
        out_shape=jax.ShapeDtypeStruct((2 * CT_DEV, DEPTH, WIDTH), BF16),
        compiler_params=params(),
        cost_estimate=cost(1 << 20, 3 << 20),
        name="stack",
    )(own, other)


def range_kernel(lanes, note_ref, here_ref, stack_ref, *refs):
    msg_refs, out_refs, turned_ref = refs[: -NX - 1], refs[-NX - 1 : -1], refs[-1]
    for ref in out_refs:
        ref[...] = jnp.zeros_like(ref)
    for k in range(8):
        spot = source(here_ref, k)
        msg_ref = msg_refs[0].at[spot] if len(msg_refs) == 1 else msg_refs[k]
        for i, z in enumerate(lanes):
            note = note_ref[spot * 8 + z]
            place = jnp.maximum(note, 0)
            col = k % 2 * CT_DEV + (place + here_ref[0]) % CT_DEV
            rows = []
            for s in range(NX):
                start = i * SIDE + (here_ref[2] + s) % NX * PART
                rows.append(msg_ref[pl.ds(pl.multiple_of(start, PART), PART)])
            tile = jnp.where(note >= 0, jnp.concatenate(rows), 0.0)
            high, low = split(tile)
            left = jnp.concatenate([high, low, high], axis=1)
            product = jnp.dot(left, stack_ref[col], preferred_element_type=F32)
            for s, ref in enumerate(out_refs):
                ref[i, place // CT_DEV] += product[s * PART : (s + 1) * PART]
            high, low = split(msg_ref[pl.ds(i * SIDE, SIDE)].T)
            turned_ref[k, i, :, pl.ds(0, SIDE)] = high
            turned_ref[k, i, :, pl.ds(SIDE, SIDE)] = low


def range_part(lanes, notes, here, msgs, weights):
    shape = [jax.ShapeDtypeStruct((len(lanes), 2, PART, WIDTH), F32)] * NX
    shape += [jax.ShapeDtypeStruct((8, len(lanes), SIDE, 2 * SIDE), BF16)]
    kernel = functools.partial(range_kernel, lanes)
    return on_chip(kernel, "range_part", (notes, here), (weights, *msgs), shape, size=1 << 22)


def corange_kernel(note_ref, here_ref, *refs):
    turned_refs, block_refs, (*out_refs, stack_ref) = refs[:2], refs[2:18], refs[18:]

    for i, ref in enumerate(block_refs):
        z = (here_ref[3] + i) % 8
        for pair in range(2):
            part = (here_ref[2] + i // 8 * 2 + pair) % NX * PART
            high, low = split(ref[pair])
            for r in range(2):
                for j, value in enumerate((high, high, low)):
                    spot = pl.ds(pl.multiple_of(j * SIDE + part, PART), PART)
                    stack_ref[z * 2 + r, spot] = value[r * PART : (r + 1) * PART]

    for ref in out_refs:
        ref[...] = jnp.zeros_like(ref)
    for k in range(8):
        spot = source(here_ref, k)
        for z in range(8):
            note = note_ref[spot * 8 + z]
            place = jnp.maximum(note, 0)
            pair = turned_refs[0][k, z] if z < SPLIT else turned_refs[1][k, z - SPLIT]
            pair = jnp.where(note >= 0, pair, jnp.zeros((), BF16))
            left = jnp.concatenate([pair, pair[:, :SIDE]], axis=1)
            right = stack_ref[z * 2 + place // CT_DEV]
            ref = out_refs[k % 2]
            ref[place % CT_DEV] += jnp.dot(left, right, preferred_element_type=F32)


def corange_part(notes, here, turned, near):
    shape = [jax.ShapeDtypeStruct((CT_DEV, SIDE, WIDTH), F32)] * 2
    scratch = [pltpu.VMEM((16, DEPTH, WIDTH), BF16)]
    arrays = (*turned, *near)
    return on_chip(corange_kernel, "corange_part", (notes, here), arrays, shape, scratch, size=1 << 22)


def gather_sum_kernel(in_ref, out_ref):
    total = in_ref[0]
    for k in range(1, 8):
        total = total + in_ref[k]
    out_ref[...] = total


def gather_sum(parts):
    shape = jax.ShapeDtypeStruct(parts.shape[1:], F32)
    return on_chip(gather_sum_kernel, "gather_sum", (), (parts,), shape)


def join_kernel(a_ref, b_ref, *out_refs):
    for k, ref in enumerate(out_refs):
        ref[...] = a_ref[k] + b_ref[k]


def join(a, b):
    shape = [jax.ShapeDtypeStruct((SIDE, WIDTH), F32)] * CT_DEV
    return on_chip(join_kernel, "join", (), (a, b), shape)


def place_kernel(here_ref, *refs):
    *in_refs, out_ref = refs
    for s, ref in enumerate(in_refs):
        out_ref[(here_ref[0] - s + 4) % 4] = ref[...]


def place(here, *arrays):
    shape = jax.ShapeDtypeStruct((4,) + arrays[0].shape, F32)
    return on_chip(place_kernel, "place", (here,), arrays, shape)


def exchange(value, axes):
    return lax.all_to_all(value, axes, split_axis=0, concat_axis=0, tiled=True)


def shifted(value, axis, step):
    n = lax.axis_size(axis)
    return lax.ppermute(value, axis, [(i, (i + step) % n) for i in range(n)])


def partner(value, k):
    pairs = []
    for i in range(8):
        pairs.append((i, (i // 2 + k // 2) % 4 * 2 + (i + k) % 2))
    return lax.ppermute(value, ("y", "c"), pairs)


def settle_kernel(here_ref, *refs):
    *in_refs, out_ref = refs
    for m, ref in enumerate(in_refs):
        x = (here_ref[0] - m + 4) % 4
        for r in range(2):
            spot = pl.ds(pl.multiple_of(r * SIDE + x * PART, PART), PART)
            out_ref[spot] = ref[pl.ds(r * PART, PART)]


def settle(here, pieces):
    shape = jax.ShapeDtypeStruct((2 * SIDE, WIDTH), F32)
    return on_chip(settle_kernel, "settle", (here,), pieces, shape)


def on_device(tiles, tile_dest, tile_row, tile_col, omega, col_scale):
    here = jnp.stack([lax.axis_index(name) for name in "ycxz"]).astype(jnp.int32)
    weights = col_scale.astype(F32)

    index = tile_dest[0, 0, :, 0] * 8 + tile_row[0, 0] * 4 + tile_col[0, 0]
    first, second = pack(here, index, tiles[0, 0])
    scaled = (omega * weights[:, None]).reshape(CT_DEV, SIDE, WIDTH)
    stacked = stack(scaled, shifted(scaled, "c", 1))

    first = exchange(first, ("y", "c"))
    for k in range(1, 8):
        second[k] = partner(second[k], k)
    notes = first[:, SPLIT * SIDE, :8].reshape(64)
    notes = notes.astype(jnp.int32)
    parts = []
    turned = []
    for lanes, msgs in ((range(SPLIT), (first,)), (range(SPLIT, 8), second)):
        *blocks, back = range_part(lanes, notes, here, msgs, stacked)
        turned.append(back)
        if parts:
            *blocks, parts[0] = lax.optimization_barrier((*blocks, parts[0]))
        part = blocks[0]
        for s in range(1, NX):
            part = part + shifted(blocks[s], "x", s)
        parts.append(part)
    part = jnp.concatenate(parts)
    piece = gather_sum(exchange(part.reshape(8, HALF, WIDTH), "z"))

    pieces = []
    for m in range(4):
        pairs = [(y * 4 + x, (x + m) % 4 * 4 + y) for y in range(4) for x in range(4)]
        pieces.append(lax.ppermute(piece, ("y", "x"), pairs))

    around = [piece] + [shifted(piece, "x", -s) for s in range(1, NX)]
    blocks = []
    for pair, up, down in ((around[:2], 4, 3), (around[2:], 3, 4)):
        block = jnp.stack(pair)
        ring = {0: block}
        for step in range(1, 5):
            if step <= up:
                ring[8 - step] = shifted(ring[(9 - step) % 8], "z", 1)
            if step <= down:
                ring[step] = shifted(ring[step - 1], "z", -1)
        blocks += [ring[k] for k in range(8)]

    own, other = corange_part(notes, here, turned, blocks)
    total = join(own, shifted(other, "c", 1))
    columns = total[0]
    for s in range(1, 4):
        columns = columns + shifted(total[s], "y", s)
    columns = columns * lax.dynamic_slice_in_dim(weights, here[0] * SIDE, SIDE, axis=0)[:, None]
    corange_local = place(here, columns, *[shifted(columns, "y", s) for s in range(1, 4)])
    corange_local = corange_local.reshape(CT_DEV * SIDE, WIDTH)
    return settle(here, pieces), corange_local


def solution(mesh):
    fine = Mesh(mesh.devices.reshape(4, 8, 4, 2), ("y", "z", "x", "c"))
    lane = ("z", "x", "c")
    placed = (
        P("y", lane, None, None, None),
        P("y", lane, None, None),
        P("y", lane, None),
        P("y", lane, None),
        P(lane, None),
        P(lane),
    )
    return jax.shard_map(
        on_device,
        mesh=fine,
        in_specs=placed,
        out_specs=(P(lane, None), P(lane, None)),
        check_vma=False,
    )
```

```python
import functools

import jax
import jax.numpy as jnp
from jax import lax
from jax.experimental import pallas as pl
from jax.experimental.pallas import tpu as pltpu
from jax.sharding import Mesh, PartitionSpec as P

SIDE = 128
WIDTH = 256
CT_DEV = 4
NX = 4
DEPTH = 3 * SIDE
PART = SIDE // 4
HALF = SIDE // 2
SPLIT = 4
VMEM = 12 * 1024 * 1024
F32 = jnp.float32
BF16 = jnp.bfloat16


def split(value):
    high = value.astype(BF16)
    low = (value - high.astype(F32)).astype(BF16)
    return high, low


def params():
    return pltpu.CompilerParams(vmem_limit_bytes=VMEM)


def cost(flops, size):
    return pl.CostEstimate(flops=flops, bytes_accessed=size, transcendentals=0)


def on_chip(kernel, name, scalars, arrays, out_shape, scratch=(), flops=1 << 20, size=1 << 20):
    many = isinstance(out_shape, list)
    vmem, smem = (pl.BlockSpec(memory_space=space) for space in (pltpu.VMEM, pltpu.SMEM))
    return pl.pallas_call(
        kernel,
        out_shape=out_shape,
        in_specs=[smem] * len(scalars) + [vmem] * len(arrays),
        out_specs=[vmem] * len(out_shape) if many else vmem,
        scratch_shapes=list(scratch),
        compiler_params=params(),
        cost_estimate=cost(flops, size),
        name=name,
    )(*scalars, *arrays)


def source(here_ref, k):
    return (here_ref[0] - k // 2 + 4) % 4 * 2 + (here_ref[1] + k) % 2


def pack_kernel(here_ref, index_ref, tiles_ref, *refs):
    out_refs, (from_ref, note_ref) = refs[:-2], refs[-2:]
    for i in range(64):
        from_ref[i] = 0
        note_ref[i] = -1

    @pl.loop(0, tiles_ref.shape[0])
    def _(t):
        index = index_ref[t]
        lane = index // 8
        z, x, c = lane // 8, lane // 2 % 4, lane % 2
        k = (x - here_ref[0] + 4) % 4 * 2 + (c + here_ref[1]) % 2
        slot = k * 8 + z
        from_ref[slot] = t
        note_ref[slot] = index // 4 % 2 * CT_DEV + (index - x + 64) % 4

    spot = lax.broadcasted_iota(jnp.int32, (8, SIDE), 1)
    for k in range(8):
        partner = (here_ref[0] + k // 2) % 4 * 2 + (here_ref[1] + k) % 2
        first_ref, second_ref = out_refs[8].at[partner], out_refs[k]

        def some(z, notes, k=k, first_ref=first_ref, second_ref=second_ref):
            slot = k * 8 + z
            start = pl.multiple_of(z * SIDE, SIDE)
            first_ref[pl.ds(start, SIDE)] = tiles_ref[from_ref[slot]]
            second_ref[pl.ds(start, SIDE)] = tiles_ref[from_ref[slot + SPLIT]]
            notes = jnp.where(spot == z, note_ref[slot], notes)
            return jnp.where(spot == z + SPLIT, note_ref[slot + SPLIT], notes)

        notes = lax.fori_loop(0, SPLIT, some, jnp.full((8, SIDE), -1, jnp.int32))
        first_ref[pl.ds(SPLIT * SIDE, 8)] = notes.astype(F32)


def pack(here, index, tiles):
    shape = [jax.ShapeDtypeStruct(((8 - SPLIT) * SIDE, SIDE), F32)] * 8
    shape += [jax.ShapeDtypeStruct((8, SPLIT * SIDE + 8, SIDE), F32)]
    scratch = [pltpu.SMEM((64,), jnp.int32)] * 2
    out = on_chip(pack_kernel, "pack", (here, index), (tiles,), shape, scratch, size=8 << 20)
    return out[8], list(out[:8])


def stack_kernel(own_ref, other_ref, out_ref):
    for i, ref in enumerate((own_ref, other_ref)):
        for k in range(CT_DEV):
            high, low = split(ref[k])
            out_ref[i * CT_DEV + k, pl.ds(0, SIDE)] = high
            out_ref[i * CT_DEV + k, pl.ds(SIDE, SIDE)] = high
            out_ref[i * CT_DEV + k, pl.ds(2 * SIDE, SIDE)] = low


def stack(own, other):
    return pl.pallas_call(
        stack_kernel,
        out_shape=jax.ShapeDtypeStruct((2 * CT_DEV, DEPTH, WIDTH), BF16),
        compiler_params=params(),
        cost_estimate=cost(1 << 20, 3 << 20),
        name="stack",
    )(own, other)


def range_kernel(first, note_ref, here_ref, stack_ref, *refs):
    msg_refs, out_refs, turned_ref = refs[: -NX - 1], refs[-NX - 1 : -1], refs[-1]
    for ref in out_refs:
        ref[...] = jnp.zeros_like(ref)

    def multiply(k, msg_ref, i, z):
        note = note_ref[source(here_ref, k) * 8 + z]
        place = jnp.maximum(note, 0)
        col = k % 2 * CT_DEV + (place + here_ref[0]) % CT_DEV
        rows = []
        for s in range(NX):
            start = i * SIDE + (here_ref[2] + s) % NX * PART
            rows.append(msg_ref[pl.ds(pl.multiple_of(start, PART), PART)])
        tile = jnp.where(note >= 0, jnp.concatenate(rows), 0.0)
        high, low = split(tile)
        left = jnp.concatenate([high, low, high], axis=1)
        product = jnp.dot(left, stack_ref[col], preferred_element_type=F32)
        for s, ref in enumerate(out_refs):
            ref[i, place // CT_DEV] += product[s * PART : (s + 1) * PART]
        high, low = split(msg_ref[pl.ds(pl.multiple_of(i * SIDE, SIDE), SIDE)].T)
        turned_ref[k, i, :, pl.ds(0, SIDE)] = high
        turned_ref[k, i, :, pl.ds(SIDE, SIDE)] = low

    if first:

        @pl.loop(0, 8)
        def _(k):
            for z in range(SPLIT):
                multiply(k, msg_refs[0].at[source(here_ref, k)], z, z)

    else:

        @pl.loop(0, 8 - SPLIT)
        def _(i):
            for k, msg_ref in enumerate(msg_refs):
                multiply(k, msg_ref, i, i + SPLIT)


def range_part(lanes, notes, here, msgs, weights):
    shape = [jax.ShapeDtypeStruct((len(lanes), 2, PART, WIDTH), F32)] * NX
    shape += [jax.ShapeDtypeStruct((8, len(lanes), SIDE, 2 * SIDE), BF16)]
    kernel = functools.partial(range_kernel, 0 in lanes)
    return on_chip(kernel, "range_part", (notes, here), (weights, *msgs), shape, size=1 << 22)


def corange_kernel(note_ref, here_ref, *refs):
    turned_refs, block_refs, (*out_refs, stack_ref) = refs[:2], refs[2:18], refs[18:]

    for i, ref in enumerate(block_refs):
        z = (here_ref[3] + i) % 8
        for pair in range(2):
            part = (here_ref[2] + i // 8 * 2 + pair) % NX * PART
            high, low = split(ref[pair])
            for r in range(2):
                for j, value in enumerate((high, high, low)):
                    spot = pl.ds(pl.multiple_of(j * SIDE + part, PART), PART)
                    stack_ref[z * 2 + r, spot] = value[r * PART : (r + 1) * PART]

    for ref in out_refs:
        ref[...] = jnp.zeros_like(ref)

    @pl.loop(0, 4)
    def _(step):
        for core, ref in enumerate(out_refs):
            k = step * 2 + core
            spot = source(here_ref, k)
            for z in range(8):
                note = note_ref[spot * 8 + z]
                place = jnp.maximum(note, 0)
                pair = turned_refs[0][k, z] if z < SPLIT else turned_refs[1][k, z - SPLIT]
                pair = jnp.where(note >= 0, pair, jnp.zeros((), BF16))
                left = jnp.concatenate([pair, pair[:, :SIDE]], axis=1)
                right = stack_ref[z * 2 + place // CT_DEV]
                ref[place % CT_DEV] += jnp.dot(left, right, preferred_element_type=F32)


def corange_part(notes, here, turned, near):
    shape = [jax.ShapeDtypeStruct((CT_DEV, SIDE, WIDTH), F32)] * 2
    scratch = [pltpu.VMEM((16, DEPTH, WIDTH), BF16)]
    arrays = (*turned, *near)
    return on_chip(corange_kernel, "corange_part", (notes, here), arrays, shape, scratch, size=1 << 22)


def gather_sum_kernel(in_ref, out_ref):
    total = in_ref[0]
    for k in range(1, 8):
        total = total + in_ref[k]
    out_ref[...] = total


def gather_sum(parts):
    shape = jax.ShapeDtypeStruct(parts.shape[1:], F32)
    return on_chip(gather_sum_kernel, "gather_sum", (), (parts,), shape)


def join_kernel(a_ref, b_ref, *out_refs):
    for k, ref in enumerate(out_refs):
        ref[...] = a_ref[k] + b_ref[k]


def join(a, b):
    shape = [jax.ShapeDtypeStruct((SIDE, WIDTH), F32)] * CT_DEV
    return on_chip(join_kernel, "join", (), (a, b), shape)


def place_kernel(here_ref, *refs):
    *in_refs, out_ref = refs
    for s, ref in enumerate(in_refs):
        out_ref[(here_ref[0] - s + 4) % 4] = ref[...]


def place(here, *arrays):
    shape = jax.ShapeDtypeStruct((4,) + arrays[0].shape, F32)
    return on_chip(place_kernel, "place", (here,), arrays, shape)


def exchange(value, axes):
    return lax.all_to_all(value, axes, split_axis=0, concat_axis=0, tiled=True)


def shifted(value, axis, step):
    n = lax.axis_size(axis)
    return lax.ppermute(value, axis, [(i, (i + step) % n) for i in range(n)])


def partner(value, k):
    pairs = []
    for i in range(8):
        pairs.append((i, (i // 2 + k // 2) % 4 * 2 + (i + k) % 2))
    return lax.ppermute(value, ("y", "c"), pairs)


def settle_kernel(here_ref, *refs):
    *in_refs, out_ref = refs
    for m, ref in enumerate(in_refs):
        x = (here_ref[0] - m + 4) % 4
        for r in range(2):
            spot = pl.ds(pl.multiple_of(r * SIDE + x * PART, PART), PART)
            out_ref[spot] = ref[pl.ds(r * PART, PART)]


def settle(here, pieces):
    shape = jax.ShapeDtypeStruct((2 * SIDE, WIDTH), F32)
    return on_chip(settle_kernel, "settle", (here,), pieces, shape)


def on_device(tiles, tile_dest, tile_row, tile_col, omega, col_scale):
    here = jnp.stack([lax.axis_index(name) for name in "ycxz"]).astype(jnp.int32)
    weights = col_scale.astype(F32)

    index = tile_dest[0, 0, :, 0] * 8 + tile_row[0, 0] * 4 + tile_col[0, 0]
    first, second = pack(here, index, tiles[0, 0])
    scaled = (omega * weights[:, None]).reshape(CT_DEV, SIDE, WIDTH)
    stacked = stack(scaled, shifted(scaled, "c", 1))

    first = exchange(first, ("y", "c"))
    for k in range(1, 8):
        second[k] = partner(second[k], k)
    notes = first[:, SPLIT * SIDE, :8].reshape(64)
    notes = notes.astype(jnp.int32)
    parts = []
    turned = []
    for lanes, msgs in ((range(SPLIT), (first,)), (range(SPLIT, 8), second)):
        *blocks, back = range_part(lanes, notes, here, msgs, stacked)
        turned.append(back)
        if parts:
            *blocks, parts[0] = lax.optimization_barrier((*blocks, parts[0]))
        part = blocks[0]
        for s in range(1, NX):
            part = part + shifted(blocks[s], "x", s)
        parts.append(part)
    part = jnp.concatenate(parts)
    piece = gather_sum(exchange(part.reshape(8, HALF, WIDTH), "z"))

    pieces = []
    for m in range(4):
        pairs = [(y * 4 + x, (x + m) % 4 * 4 + y) for y in range(4) for x in range(4)]
        pieces.append(lax.ppermute(piece, ("y", "x"), pairs))

    around = [piece] + [shifted(piece, "x", -s) for s in range(1, NX)]
    blocks = []
    for pair, up, down in ((around[:2], 4, 3), (around[2:], 3, 4)):
        block = jnp.stack(pair)
        ring = {0: block}
        for step in range(1, 5):
            if step <= up:
                ring[8 - step] = shifted(ring[(9 - step) % 8], "z", 1)
            if step <= down:
                ring[step] = shifted(ring[step - 1], "z", -1)
        blocks += [ring[k] for k in range(8)]

    own, other = corange_part(notes, here, turned, blocks)
    total = join(own, shifted(other, "c", 1))
    columns = total[0]
    for s in range(1, 4):
        columns = columns + shifted(total[s], "y", s)
    columns = columns * lax.dynamic_slice_in_dim(weights, here[0] * SIDE, SIDE, axis=0)[:, None]
    corange_local = place(here, columns, *[shifted(columns, "y", s) for s in range(1, 4)])
    corange_local = corange_local.reshape(CT_DEV * SIDE, WIDTH)
    return settle(here, pieces), corange_local


def solution(mesh):
    fine = Mesh(mesh.devices.reshape(4, 8, 4, 2), ("y", "z", "x", "c"))
    lane = ("z", "x", "c")
    placed = (
        P("y", lane, None, None, None),
        P("y", lane, None, None),
        P("y", lane, None),
        P("y", lane, None),
        P(lane, None),
        P(lane),
    )
    return jax.shard_map(
        on_device,
        mesh=fine,
        in_specs=placed,
        out_specs=(P(lane, None), P(lane, None)),
        check_vma=False,
    )
```

```python
import functools

import jax
import jax.numpy as jnp
from jax import lax
from jax.experimental import pallas as pl
from jax.experimental.pallas import tpu as pltpu
from jax.sharding import Mesh, PartitionSpec as P

SIDE = 128
WIDTH = 256
CT_DEV = 4
NX = 4
DEPTH = 3 * SIDE
PART = SIDE // 4
HALF = SIDE // 2
SPLIT = 4
VMEM = 12 * 1024 * 1024
F32 = jnp.float32
BF16 = jnp.bfloat16


def split(value):
    high = value.astype(BF16)
    low = (value - high.astype(F32)).astype(BF16)
    return high, low


def params():
    return pltpu.CompilerParams(vmem_limit_bytes=VMEM)


def cost(flops, size):
    return pl.CostEstimate(flops=flops, bytes_accessed=size, transcendentals=0)


def on_chip(kernel, name, scalars, arrays, out_shape, scratch=(), flops=1 << 20, size=1 << 20):
    many = isinstance(out_shape, list)
    vmem, smem = (pl.BlockSpec(memory_space=space) for space in (pltpu.VMEM, pltpu.SMEM))
    return pl.pallas_call(
        kernel,
        out_shape=out_shape,
        in_specs=[smem] * len(scalars) + [vmem] * len(arrays),
        out_specs=[vmem] * len(out_shape) if many else vmem,
        scratch_shapes=list(scratch),
        compiler_params=params(),
        cost_estimate=cost(flops, size),
        name=name,
    )(*scalars, *arrays)


def source(here_ref, k):
    return (here_ref[0] - k // 2 + 4) % 4 * 2 + (here_ref[1] + k) % 2


def find_tiles(here_ref, index_ref, from_ref, note_ref):
    for i in range(64):
        from_ref[i] = 0
        if note_ref is not None:
            note_ref[i] = -1

    @pl.loop(0, index_ref.shape[0])
    def _(t):
        index = index_ref[t]
        lane = index // 8
        z, x, c = lane // 8, lane // 2 % 4, lane % 2
        k = (x - here_ref[0] + 4) % 4 * 2 + (c + here_ref[1]) % 2
        slot = k * 8 + z
        from_ref[slot] = t
        if note_ref is not None:
            note_ref[slot] = index // 4 % 2 * CT_DEV + (index - x + 64) % 4


def first_kernel(here_ref, index_ref, tiles_ref, out_ref, from_ref, note_ref):
    find_tiles(here_ref, index_ref, from_ref, note_ref)
    spot = lax.broadcasted_iota(jnp.int32, (8, SIDE), 1)

    @pl.loop(0, 8)
    def _(k):
        ref = out_ref.at[(here_ref[0] + k // 2) % 4 * 2 + (here_ref[1] + k) % 2]
        notes = jnp.full((8, SIDE), -1, jnp.int32)
        for z in range(8):
            if z < SPLIT:
                ref[pl.ds(z * SIDE, SIDE)] = tiles_ref[from_ref[k * 8 + z]]
            notes = jnp.where(spot == z, note_ref[k * 8 + z], notes)
        ref[pl.ds(SPLIT * SIDE, 8)] = notes.astype(F32)


def pack_first(here, index, tiles):
    shape = jax.ShapeDtypeStruct((8, SPLIT * SIDE + 8, SIDE), F32)
    scratch = [pltpu.SMEM((64,), jnp.int32)] * 2
    return on_chip(first_kernel, "pack_first", (here, index), (tiles,), shape, scratch)


def second_kernel(here_ref, index_ref, tiles_ref, omega_ref, *refs):
    out_refs, from_ref = refs[:-1], refs[-1]
    find_tiles(here_ref, index_ref, from_ref, None)

    @pl.loop(0, 8 - SPLIT)
    def _(i):
        for k, ref in enumerate(out_refs):
            start = pl.multiple_of(i * SIDE, SIDE)
            ref[pl.ds(start, SIDE)] = tiles_ref[from_ref[k * 8 + SPLIT + i]]

    start, count = (8 - SPLIT) * SIDE, CT_DEV * SIDE
    out_refs[1][pl.ds(start, count)] = omega_ref[:, pl.ds(0, SIDE)]
    out_refs[1][pl.ds(start + count, count)] = omega_ref[:, pl.ds(SIDE, SIDE)]


def pack_second(here, index, tiles, omega):
    rows = [(8 - SPLIT) * SIDE] * 8
    rows[1] += 2 * CT_DEV * SIDE
    shape = [jax.ShapeDtypeStruct((count, SIDE), F32) for count in rows]
    scratch = [pltpu.SMEM((64,), jnp.int32)]
    arrays = (tiles, omega)
    return list(on_chip(second_kernel, "pack_second", (here, index), arrays, shape, scratch))


def stack_kernel(own_ref, msg_ref, out_ref):
    start, count = (8 - SPLIT) * SIDE, CT_DEV * SIDE
    for k in range(CT_DEV):
        own = own_ref[pl.ds(k * SIDE, SIDE)]
        other = [msg_ref[pl.ds(start + i * count + k * SIDE, SIDE)] for i in range(2)]
        for i, value in enumerate((own, jnp.concatenate(other, axis=1))):
            high, low = split(value)
            out_ref[i * CT_DEV + k, pl.ds(0, SIDE)] = high
            out_ref[i * CT_DEV + k, pl.ds(SIDE, SIDE)] = high
            out_ref[i * CT_DEV + k, pl.ds(2 * SIDE, SIDE)] = low


def stack(own, msg):
    shape = jax.ShapeDtypeStruct((2 * CT_DEV, DEPTH, WIDTH), BF16)
    return on_chip(stack_kernel, "stack", (), (own, msg), shape, size=3 << 20)


def range_kernel(first, note_ref, here_ref, stack_ref, *refs):
    msg_refs, out_refs, turned_ref = refs[: -NX - 1], refs[-NX - 1 : -1], refs[-1]
    for ref in out_refs:
        ref[...] = jnp.zeros_like(ref)

    def multiply(k, msg_ref, i, z):
        note = note_ref[source(here_ref, k) * 8 + z]
        place = jnp.maximum(note, 0)
        col = k % 2 * CT_DEV + (place + here_ref[0]) % CT_DEV
        rows = []
        for s in range(NX):
            start = i * SIDE + (here_ref[2] + s) % NX * PART
            rows.append(msg_ref[pl.ds(pl.multiple_of(start, PART), PART)])
        tile = jnp.where(note >= 0, jnp.concatenate(rows), 0.0)
        high, low = split(tile)
        left = jnp.concatenate([high, low, high], axis=1)
        product = jnp.dot(left, stack_ref[col], preferred_element_type=F32)
        for s, ref in enumerate(out_refs):
            ref[i, place // CT_DEV] += product[s * PART : (s + 1) * PART]
        high, low = split(msg_ref[pl.ds(pl.multiple_of(i * SIDE, SIDE), SIDE)].T)
        turned_ref[k, i, :, pl.ds(0, SIDE)] = high
        turned_ref[k, i, :, pl.ds(SIDE, SIDE)] = low

    if first:

        @pl.loop(0, 8)
        def _(k):
            for z in range(SPLIT):
                multiply(k, msg_refs[0].at[source(here_ref, k)], z, z)

    else:

        @pl.loop(0, 8 - SPLIT)
        def _(i):
            for k, msg_ref in enumerate(msg_refs):
                multiply(k, msg_ref, i, i + SPLIT)


def range_part(lanes, notes, here, msgs, weights):
    shape = [jax.ShapeDtypeStruct((len(lanes), 2, PART, WIDTH), F32)] * NX
    shape += [jax.ShapeDtypeStruct((8, len(lanes), SIDE, 2 * SIDE), BF16)]
    kernel = functools.partial(range_kernel, 0 in lanes)
    return on_chip(kernel, "range_part", (notes, here), (weights, *msgs), shape, size=1 << 22)


def corange_kernel(note_ref, here_ref, *refs):
    turned_refs, block_refs, (*out_refs, stack_ref) = refs[:2], refs[2:18], refs[18:]

    for i, ref in enumerate(block_refs):
        z = (here_ref[3] + i) % 8
        for pair in range(2):
            part = (here_ref[2] + i // 8 * 2 + pair) % NX * PART
            high, low = split(ref[pair])
            for r in range(2):
                for j, value in enumerate((high, high, low)):
                    spot = pl.ds(pl.multiple_of(j * SIDE + part, PART), PART)
                    stack_ref[z * 2 + r, spot] = value[r * PART : (r + 1) * PART]

    for ref in out_refs:
        ref[...] = jnp.zeros_like(ref)

    @pl.loop(0, 4)
    def _(step):
        for core, ref in enumerate(out_refs):
            k = step * 2 + core
            spot = source(here_ref, k)
            for z in range(8):
                note = note_ref[spot * 8 + z]
                place = jnp.maximum(note, 0)
                pair = turned_refs[0][k, z] if z < SPLIT else turned_refs[1][k, z - SPLIT]
                pair = jnp.where(note >= 0, pair, jnp.zeros((), BF16))
                left = jnp.concatenate([pair, pair[:, :SIDE]], axis=1)
                right = stack_ref[z * 2 + place // CT_DEV]
                ref[place % CT_DEV] += jnp.dot(left, right, preferred_element_type=F32)


def corange_part(notes, here, turned, near):
    shape = [jax.ShapeDtypeStruct((CT_DEV, SIDE, WIDTH), F32)] * 2
    scratch = [pltpu.VMEM((16, DEPTH, WIDTH), BF16)]
    arrays = (*turned, *near)
    return on_chip(corange_kernel, "corange_part", (notes, here), arrays, shape, scratch, size=1 << 22)


def gather_sum_kernel(in_ref, out_ref):
    total = in_ref[0]
    for k in range(1, 8):
        total = total + in_ref[k]
    out_ref[...] = total


def gather_sum(parts):
    shape = jax.ShapeDtypeStruct(parts.shape[1:], F32)
    return on_chip(gather_sum_kernel, "gather_sum", (), (parts,), shape)


def join_kernel(a_ref, b_ref, *out_refs):
    for k, ref in enumerate(out_refs):
        ref[...] = a_ref[k] + b_ref[k]


def join(a, b):
    shape = [jax.ShapeDtypeStruct((SIDE, WIDTH), F32)] * CT_DEV
    return on_chip(join_kernel, "join", (), (a, b), shape)


def place_kernel(here_ref, *refs):
    *in_refs, out_ref = refs
    for s, ref in enumerate(in_refs):
        out_ref[(here_ref[0] - s + 4) % 4] = ref[...]


def place(here, *arrays):
    shape = jax.ShapeDtypeStruct((4,) + arrays[0].shape, F32)
    return on_chip(place_kernel, "place", (here,), arrays, shape)


def exchange(value, axes):
    return lax.all_to_all(value, axes, split_axis=0, concat_axis=0, tiled=True)


def shifted(value, axis, step):
    n = lax.axis_size(axis)
    return lax.ppermute(value, axis, [(i, (i + step) % n) for i in range(n)])


def partner(value, k):
    pairs = []
    for i in range(8):
        pairs.append((i, (i // 2 + k // 2) % 4 * 2 + (i + k) % 2))
    return lax.ppermute(value, ("y", "c"), pairs)


def settle_kernel(here_ref, *refs):
    *in_refs, out_ref = refs
    for s, ref in enumerate(in_refs):
        x = (here_ref[2] + s) % NX
        for r in range(2):
            spot = pl.ds(pl.multiple_of(r * SIDE + x * PART, PART), PART)
            out_ref[spot] = ref[pl.ds(r * PART, PART)]


def settle(here, pieces):
    shape = jax.ShapeDtypeStruct((2 * SIDE, WIDTH), F32)
    return on_chip(settle_kernel, "settle", (here,), pieces, shape)


def choose_kernel(here_ref, *refs):
    *in_refs, out_ref = refs
    for s, ref in enumerate(in_refs):

        @pl.when((here_ref[0] - here_ref[2] + 4) % 4 == s)
        def _():
            out_ref[...] = ref[...]


def choose(here, arrays):
    shape = jax.ShapeDtypeStruct((2 * SIDE, WIDTH), F32)
    return on_chip(choose_kernel, "choose", (here,), arrays, shape)


def on_device(tiles, tile_dest, tile_row, tile_col, omega, col_scale):
    here = jnp.stack([lax.axis_index(name) for name in "ycxz"]).astype(jnp.int32)
    weights = col_scale.astype(F32)

    index = tile_dest[0, 0, :, 0] * 8 + tile_row[0, 0] * 4 + tile_col[0, 0]
    scaled = omega * weights[:, None]
    first = exchange(pack_first(here, index, tiles[0, 0]), ("y", "c"))
    second = pack_second(here, index, tiles[0, 0], scaled)
    for k in range(1, 8):
        second[k] = partner(second[k], k)
    stacked = stack(scaled, second[1])
    notes = first[:, SPLIT * SIDE, :8].reshape(64)
    notes = notes.astype(jnp.int32)
    parts = []
    turned = []
    for lanes, msgs in ((range(SPLIT), (first,)), (range(SPLIT, 8), second)):
        *blocks, back = range_part(lanes, notes, here, msgs, stacked)
        turned.append(back)
        if parts:
            *blocks, parts[0] = lax.optimization_barrier((*blocks, parts[0]))
        part = blocks[0]
        for s in range(1, NX):
            part = part + shifted(blocks[s], "x", s)
        parts.append(part)
    part = jnp.concatenate(parts)
    piece = gather_sum(exchange(part.reshape(8, HALF, WIDTH), "z"))

    around = [piece] + [shifted(piece, "x", -s) for s in range(1, NX)]
    lane = [settle(here, around)]
    for s in range(1, 4):
        pairs = [(x * 4 + x, (x + s) % 4 * 4 + x) for x in range(4)]
        lane.append(lax.ppermute(lane[0], ("y", "x"), pairs))
    blocks = []
    for pair, up, down in ((around[:2], 4, 3), (around[2:], 3, 4)):
        block = jnp.stack(pair)
        ring = {0: block}
        for step in range(1, 5):
            if step <= up:
                ring[8 - step] = shifted(ring[(9 - step) % 8], "z", 1)
            if step <= down:
                ring[step] = shifted(ring[step - 1], "z", -1)
        blocks += [ring[k] for k in range(8)]

    blocks[4], *lane[1:] = lax.optimization_barrier((blocks[4], *lane[1:]))
    own, other = corange_part(notes, here, turned, blocks)
    total = join(own, shifted(other, "c", 1))
    columns = total[0]
    for s in range(1, 4):
        columns = columns + shifted(total[s], "y", s)
    columns = columns * lax.dynamic_slice_in_dim(weights, here[0] * SIDE, SIDE, axis=0)[:, None]
    corange_local = place(here, columns, *[shifted(columns, "y", s) for s in range(1, 4)])
    corange_local = corange_local.reshape(CT_DEV * SIDE, WIDTH)
    return choose(here, lane), corange_local


def solution(mesh):
    fine = Mesh(mesh.devices.reshape(4, 8, 4, 2), ("y", "z", "x", "c"))
    lane = ("z", "x", "c")
    placed = (
        P("y", lane, None, None, None),
        P("y", lane, None, None),
        P("y", lane, None),
        P("y", lane, None),
        P(lane, None),
        P(lane),
    )
    return jax.shard_map(
        on_device,
        mesh=fine,
        in_specs=placed,
        out_specs=(P(lane, None), P(lane, None)),
        check_vma=False,
    )
```

```python
import functools

import jax
import jax.numpy as jnp
from jax import lax
from jax.experimental import pallas as pl
from jax.experimental.pallas import tpu as pltpu
from jax.sharding import Mesh, PartitionSpec as P

SIDE = 128
WIDTH = 256
CT_DEV = 4
NX = 4
DEPTH = 3 * SIDE
PART = SIDE // 4
HALF = SIDE // 2
SPLIT = 5
VMEM = 12 * 1024 * 1024
F32 = jnp.float32
BF16 = jnp.bfloat16


def split(value):
    high = value.astype(BF16)
    low = (value - high.astype(F32)).astype(BF16)
    return high, low


def params():
    return pltpu.CompilerParams(vmem_limit_bytes=VMEM)


def cost(flops, size):
    return pl.CostEstimate(flops=flops, bytes_accessed=size, transcendentals=0)


def on_chip(kernel, name, scalars, arrays, out_shape, scratch=(), flops=1 << 20, size=1 << 20):
    many = isinstance(out_shape, list)
    vmem, smem = (pl.BlockSpec(memory_space=space) for space in (pltpu.VMEM, pltpu.SMEM))
    return pl.pallas_call(
        kernel,
        out_shape=out_shape,
        in_specs=[smem] * len(scalars) + [vmem] * len(arrays),
        out_specs=[vmem] * len(out_shape) if many else vmem,
        scratch_shapes=list(scratch),
        compiler_params=params(),
        cost_estimate=cost(flops, size),
        name=name,
    )(*scalars, *arrays)


def source(here_ref, k):
    return (here_ref[0] - k // 2 + 4) % 4 * 2 + (here_ref[1] + k) % 2


def find_tiles(here_ref, index_ref, from_ref, note_ref):
    for i in range(64):
        from_ref[i] = 0
        if note_ref is not None:
            note_ref[i] = -1

    @pl.loop(0, index_ref.shape[0])
    def _(t):
        index = index_ref[t]
        lane = index // 8
        z, x, c = lane // 8, lane // 2 % 4, lane % 2
        k = (x - here_ref[0] + 4) % 4 * 2 + (c + here_ref[1]) % 2
        slot = k * 8 + z
        from_ref[slot] = t
        if note_ref is not None:
            note_ref[slot] = index // 4 % 2 * CT_DEV + (index - x + 64) % 4


def first_kernel(here_ref, index_ref, tiles_ref, out_ref, from_ref, note_ref):
    find_tiles(here_ref, index_ref, from_ref, note_ref)
    spot = lax.broadcasted_iota(jnp.int32, (8, SIDE), 1)

    @pl.loop(0, 8)
    def _(k):
        ref = out_ref.at[(here_ref[0] + k // 2) % 4 * 2 + (here_ref[1] + k) % 2]
        notes = jnp.full((8, SIDE), -1, jnp.int32)
        for z in range(8):
            if z < SPLIT:
                ref[pl.ds(z * SIDE, SIDE)] = tiles_ref[from_ref[k * 8 + z]]
            notes = jnp.where(spot == z, note_ref[k * 8 + z], notes)
        ref[pl.ds(SPLIT * SIDE, 8)] = notes.astype(F32)


def pack_first(here, index, tiles):
    shape = jax.ShapeDtypeStruct((8, SPLIT * SIDE + 8, SIDE), F32)
    scratch = [pltpu.SMEM((64,), jnp.int32)] * 2
    return on_chip(first_kernel, "pack_first", (here, index), (tiles,), shape, scratch)


def second_kernel(here_ref, index_ref, tiles_ref, omega_ref, *refs):
    out_refs, from_ref = refs[:-1], refs[-1]
    find_tiles(here_ref, index_ref, from_ref, None)

    @pl.loop(0, 8 - SPLIT)
    def _(i):
        for k, ref in enumerate(out_refs):
            start = pl.multiple_of(i * SIDE, SIDE)
            ref[pl.ds(start, SIDE)] = tiles_ref[from_ref[k * 8 + SPLIT + i]]

    start, count = (8 - SPLIT) * SIDE, CT_DEV * SIDE
    out_refs[1][pl.ds(start, count)] = omega_ref[:, pl.ds(0, SIDE)]
    out_refs[1][pl.ds(start + count, count)] = omega_ref[:, pl.ds(SIDE, SIDE)]


def pack_second(here, index, tiles, omega):
    rows = [(8 - SPLIT) * SIDE] * 8
    rows[1] += 2 * CT_DEV * SIDE
    shape = [jax.ShapeDtypeStruct((count, SIDE), F32) for count in rows]
    scratch = [pltpu.SMEM((64,), jnp.int32)]
    arrays = (tiles, omega)
    return list(on_chip(second_kernel, "pack_second", (here, index), arrays, shape, scratch))


def stack_kernel(own_ref, msg_ref, out_ref):
    start, count = (8 - SPLIT) * SIDE, CT_DEV * SIDE
    for k in range(CT_DEV):
        own = own_ref[pl.ds(k * SIDE, SIDE)]
        other = [msg_ref[pl.ds(start + i * count + k * SIDE, SIDE)] for i in range(2)]
        for i, value in enumerate((own, jnp.concatenate(other, axis=1))):
            high, low = split(value)
            out_ref[i * CT_DEV + k, pl.ds(0, SIDE)] = high
            out_ref[i * CT_DEV + k, pl.ds(SIDE, SIDE)] = high
            out_ref[i * CT_DEV + k, pl.ds(2 * SIDE, SIDE)] = low


def stack(own, msg):
    shape = jax.ShapeDtypeStruct((2 * CT_DEV, DEPTH, WIDTH), BF16)
    return on_chip(stack_kernel, "stack", (), (own, msg), shape, size=3 << 20)


def range_kernel(first, note_ref, here_ref, stack_ref, *refs):
    msg_refs, out_refs, turned_ref = refs[: -NX - 1], refs[-NX - 1 : -1], refs[-1]
    for ref in out_refs:
        ref[...] = jnp.zeros_like(ref)

    def multiply(k, msg_ref, i, z):
        note = note_ref[source(here_ref, k) * 8 + z]
        place = jnp.maximum(note, 0)
        col = k % 2 * CT_DEV + (place + here_ref[0]) % CT_DEV
        rows = []
        for s in range(NX):
            start = i * SIDE + (here_ref[2] + s) % NX * PART
            rows.append(msg_ref[pl.ds(pl.multiple_of(start, PART), PART)])
        tile = jnp.where(note >= 0, jnp.concatenate(rows), 0.0)
        high, low = split(tile)
        left = jnp.concatenate([high, low, high], axis=1)
        product = jnp.dot(left, stack_ref[col], preferred_element_type=F32)
        for s, ref in enumerate(out_refs):
            ref[i, place // CT_DEV] += product[s * PART : (s + 1) * PART]
        high, low = split(msg_ref[pl.ds(pl.multiple_of(i * SIDE, SIDE), SIDE)].T)
        turned_ref[k, i, :, pl.ds(0, SIDE)] = high
        turned_ref[k, i, :, pl.ds(SIDE, SIDE)] = low

    if first:

        @pl.loop(0, 8)
        def _(k):
            for z in range(SPLIT):
                multiply(k, msg_refs[0].at[source(here_ref, k)], z, z)

    else:

        @pl.loop(0, 8 - SPLIT)
        def _(i):
            for k, msg_ref in enumerate(msg_refs):
                multiply(k, msg_ref, i, i + SPLIT)


def range_part(lanes, notes, here, msgs, weights):
    shape = [jax.ShapeDtypeStruct((len(lanes), 2, PART, WIDTH), F32)] * NX
    shape += [jax.ShapeDtypeStruct((8, len(lanes), SIDE, 2 * SIDE), BF16)]
    kernel = functools.partial(range_kernel, 0 in lanes)
    return on_chip(kernel, "range_part", (notes, here), (weights, *msgs), shape, size=1 << 22)


def corange_kernel(note_ref, here_ref, *refs):
    turned_refs, block_refs, (*out_refs, stack_ref) = refs[:2], refs[2:18], refs[18:]

    for i, ref in enumerate(block_refs):
        z = (here_ref[3] + i) % 8
        for pair in range(2):
            part = (here_ref[2] + i // 8 * 2 + pair) % NX * PART
            high, low = split(ref[pair])
            for r in range(2):
                for j, value in enumerate((high, high, low)):
                    spot = pl.ds(pl.multiple_of(j * SIDE + part, PART), PART)
                    stack_ref[z * 2 + r, spot] = value[r * PART : (r + 1) * PART]

    for ref in out_refs:
        ref[...] = jnp.zeros_like(ref)

    @pl.loop(0, 4)
    def _(step):
        for core, ref in enumerate(out_refs):
            k = step * 2 + core
            spot = source(here_ref, k)
            for z in range(8):
                note = note_ref[spot * 8 + z]
                place = jnp.maximum(note, 0)
                pair = turned_refs[0][k, z] if z < SPLIT else turned_refs[1][k, z - SPLIT]
                pair = jnp.where(note >= 0, pair, jnp.zeros((), BF16))
                left = jnp.concatenate([pair, pair[:, :SIDE]], axis=1)
                right = stack_ref[z * 2 + place // CT_DEV]
                ref[place % CT_DEV] += jnp.dot(left, right, preferred_element_type=F32)


def corange_part(notes, here, turned, near):
    shape = [jax.ShapeDtypeStruct((CT_DEV, SIDE, WIDTH), F32)] * 2
    scratch = [pltpu.VMEM((16, DEPTH, WIDTH), BF16)]
    arrays = (*turned, *near)
    return on_chip(corange_kernel, "corange_part", (notes, here), arrays, shape, scratch, size=1 << 22)


def gather_sum_kernel(in_ref, out_ref):
    total = in_ref[0]
    for k in range(1, 8):
        total = total + in_ref[k]
    out_ref[...] = total


def gather_sum(parts):
    shape = jax.ShapeDtypeStruct(parts.shape[1:], F32)
    return on_chip(gather_sum_kernel, "gather_sum", (), (parts,), shape)


def join_kernel(a_ref, b_ref, *out_refs):
    for k, ref in enumerate(out_refs):
        ref[...] = a_ref[k] + b_ref[k]


def join(a, b):
    shape = [jax.ShapeDtypeStruct((SIDE, WIDTH), F32)] * CT_DEV
    return on_chip(join_kernel, "join", (), (a, b), shape)


def place_kernel(here_ref, *refs):
    *in_refs, out_ref = refs
    for s, ref in enumerate(in_refs):
        out_ref[(here_ref[0] - s + 4) % 4] = ref[...]


def place(here, *arrays):
    shape = jax.ShapeDtypeStruct((4,) + arrays[0].shape, F32)
    return on_chip(place_kernel, "place", (here,), arrays, shape)


def exchange(value, axes):
    return lax.all_to_all(value, axes, split_axis=0, concat_axis=0, tiled=True)


def shifted(value, axis, step):
    n = lax.axis_size(axis)
    return lax.ppermute(value, axis, [(i, (i + step) % n) for i in range(n)])


def partner(value, k):
    pairs = []
    for i in range(8):
        pairs.append((i, (i // 2 + k // 2) % 4 * 2 + (i + k) % 2))
    return lax.ppermute(value, ("y", "c"), pairs)


def settle_kernel(here_ref, *refs):
    *in_refs, out_ref = refs
    for s, ref in enumerate(in_refs):
        x = (here_ref[2] + s) % NX
        for r in range(2):
            spot = pl.ds(pl.multiple_of(r * SIDE + x * PART, PART), PART)
            out_ref[spot] = ref[pl.ds(r * PART, PART)]


def settle(here, pieces):
    shape = jax.ShapeDtypeStruct((2 * SIDE, WIDTH), F32)
    return on_chip(settle_kernel, "settle", (here,), pieces, shape)


def choose_kernel(here_ref, *refs):
    *in_refs, out_ref = refs
    for s, ref in enumerate(in_refs):

        @pl.when((here_ref[0] - here_ref[2] + 4) % 4 == s)
        def _():
            out_ref[...] = ref[...]


def choose(here, arrays):
    shape = jax.ShapeDtypeStruct((2 * SIDE, WIDTH), F32)
    return on_chip(choose_kernel, "choose", (here,), arrays, shape)


def on_device(tiles, tile_dest, tile_row, tile_col, omega, col_scale):
    here = jnp.stack([lax.axis_index(name) for name in "ycxz"]).astype(jnp.int32)
    weights = col_scale.astype(F32)

    index = tile_dest[0, 0, :, 0] * 8 + tile_row[0, 0] * 4 + tile_col[0, 0]
    scaled = omega * weights[:, None]
    first = exchange(pack_first(here, index, tiles[0, 0]), ("y", "c"))
    second = pack_second(here, index, tiles[0, 0], scaled)
    for k in range(1, 8):
        second[k] = partner(second[k], k)
    stacked = stack(scaled, second[1])
    notes = first[:, SPLIT * SIDE, :8].reshape(64)
    notes = notes.astype(jnp.int32)
    parts = []
    turned = []
    for lanes, msgs in ((range(SPLIT), (first,)), (range(SPLIT, 8), second)):
        *blocks, back = range_part(lanes, notes, here, msgs, stacked)
        turned.append(back)
        if parts:
            *blocks, parts[0] = lax.optimization_barrier((*blocks, parts[0]))
        part = blocks[0]
        for s in range(1, NX):
            part = part + shifted(blocks[s], "x", s)
        parts.append(part)
    part = jnp.concatenate(parts)
    piece = gather_sum(exchange(part.reshape(8, HALF, WIDTH), "z"))

    around = [piece] + [shifted(piece, "x", -s) for s in range(1, NX)]
    lane = [settle(here, around)]
    for s in range(1, 4):
        pairs = [(x * 4 + x, (x + s) % 4 * 4 + x) for x in range(4)]
        lane.append(lax.ppermute(lane[0], ("y", "x"), pairs))
    blocks = []
    for pair, up, down in ((around[:2], 4, 3), (around[2:], 3, 4)):
        block = jnp.stack(pair)
        ring = {0: block}
        for step in range(1, 5):
            if step <= up:
                ring[8 - step] = shifted(ring[(9 - step) % 8], "z", 1)
            if step <= down:
                ring[step] = shifted(ring[step - 1], "z", -1)
        blocks += [ring[k] for k in range(8)]

    blocks[4], *lane[1:] = lax.optimization_barrier((blocks[4], *lane[1:]))
    own, other = corange_part(notes, here, turned, blocks)
    total = join(own, shifted(other, "c", 1))
    columns = total[0]
    for s in range(1, 4):
        columns = columns + shifted(total[s], "y", s)
    columns = columns * lax.dynamic_slice_in_dim(weights, here[0] * SIDE, SIDE, axis=0)[:, None]
    corange_local = place(here, columns, *[shifted(columns, "y", s) for s in range(1, 4)])
    corange_local = corange_local.reshape(CT_DEV * SIDE, WIDTH)
    return choose(here, lane), corange_local


def solution(mesh):
    fine = Mesh(mesh.devices.reshape(4, 8, 4, 2), ("y", "z", "x", "c"))
    lane = ("z", "x", "c")
    placed = (
        P("y", lane, None, None, None),
        P("y", lane, None, None),
        P("y", lane, None),
        P("y", lane, None),
        P(lane, None),
        P(lane),
    )
    return jax.shard_map(
        on_device,
        mesh=fine,
        in_specs=placed,
        out_specs=(P(lane, None), P(lane, None)),
        check_vma=False,
    )
```

```python
import functools

import jax
import jax.numpy as jnp
from jax import lax
from jax.experimental import pallas as pl
from jax.experimental.pallas import tpu as pltpu
from jax.sharding import Mesh, PartitionSpec as P

SIDE = 128
WIDTH = 256
CT_DEV = 4
NX = 4
DEPTH = 3 * SIDE
PART = SIDE // 4
HALF = SIDE // 2
SPLIT = 6
VMEM = 12 * 1024 * 1024
F32 = jnp.float32
BF16 = jnp.bfloat16


def split(value):
    high = value.astype(BF16)
    low = (value - high.astype(F32)).astype(BF16)
    return high, low


def params():
    return pltpu.CompilerParams(vmem_limit_bytes=VMEM)


def cost(flops, size):
    return pl.CostEstimate(flops=flops, bytes_accessed=size, transcendentals=0)


def on_chip(kernel, name, scalars, arrays, out_shape, scratch=(), flops=1 << 20, size=1 << 20):
    many = isinstance(out_shape, list)
    vmem, smem = (pl.BlockSpec(memory_space=space) for space in (pltpu.VMEM, pltpu.SMEM))
    return pl.pallas_call(
        kernel,
        out_shape=out_shape,
        in_specs=[smem] * len(scalars) + [vmem] * len(arrays),
        out_specs=[vmem] * len(out_shape) if many else vmem,
        scratch_shapes=list(scratch),
        compiler_params=params(),
        cost_estimate=cost(flops, size),
        name=name,
    )(*scalars, *arrays)


def source(here_ref, k):
    return (here_ref[0] - k // 2 + 4) % 4 * 2 + (here_ref[1] + k) % 2


def find_tiles(here_ref, index_ref, from_ref, note_ref):
    for i in range(64):
        from_ref[i] = 0
        if note_ref is not None:
            note_ref[i] = -1

    @pl.loop(0, index_ref.shape[0])
    def _(t):
        index = index_ref[t]
        lane = index // 8
        z, x, c = lane // 8, lane // 2 % 4, lane % 2
        k = (x - here_ref[0] + 4) % 4 * 2 + (c + here_ref[1]) % 2
        slot = k * 8 + z
        from_ref[slot] = t
        if note_ref is not None:
            note_ref[slot] = index // 4 % 2 * CT_DEV + (index - x + 64) % 4


def first_kernel(here_ref, index_ref, tiles_ref, out_ref, from_ref, note_ref):
    find_tiles(here_ref, index_ref, from_ref, note_ref)
    spot = lax.broadcasted_iota(jnp.int32, (8, SIDE), 1)

    @pl.loop(0, 8)
    def _(k):
        ref = out_ref.at[(here_ref[0] + k // 2) % 4 * 2 + (here_ref[1] + k) % 2]
        notes = jnp.full((8, SIDE), -1, jnp.int32)
        for z in range(8):
            if z < SPLIT:
                ref[pl.ds(z * SIDE, SIDE)] = tiles_ref[from_ref[k * 8 + z]]
            notes = jnp.where(spot == z, note_ref[k * 8 + z], notes)
        ref[pl.ds(SPLIT * SIDE, 8)] = notes.astype(F32)


def pack_first(here, index, tiles):
    shape = jax.ShapeDtypeStruct((8, SPLIT * SIDE + 8, SIDE), F32)
    scratch = [pltpu.SMEM((64,), jnp.int32)] * 2
    return on_chip(first_kernel, "pack_first", (here, index), (tiles,), shape, scratch)


def second_kernel(here_ref, index_ref, tiles_ref, omega_ref, *refs):
    out_refs, from_ref = refs[:-1], refs[-1]
    find_tiles(here_ref, index_ref, from_ref, None)

    @pl.loop(0, 8 - SPLIT)
    def _(i):
        for k, ref in enumerate(out_refs):
            start = pl.multiple_of(i * SIDE, SIDE)
            ref[pl.ds(start, SIDE)] = tiles_ref[from_ref[k * 8 + SPLIT + i]]

    start, count = (8 - SPLIT) * SIDE, CT_DEV * SIDE
    out_refs[1][pl.ds(start, count)] = omega_ref[:, pl.ds(0, SIDE)]
    out_refs[1][pl.ds(start + count, count)] = omega_ref[:, pl.ds(SIDE, SIDE)]


def pack_second(here, index, tiles, omega):
    rows = [(8 - SPLIT) * SIDE] * 8
    rows[1] += 2 * CT_DEV * SIDE
    shape = [jax.ShapeDtypeStruct((count, SIDE), F32) for count in rows]
    scratch = [pltpu.SMEM((64,), jnp.int32)]
    arrays = (tiles, omega)
    return list(on_chip(second_kernel, "pack_second", (here, index), arrays, shape, scratch))


def stack_kernel(own_ref, msg_ref, out_ref):
    start, count = (8 - SPLIT) * SIDE, CT_DEV * SIDE
    for k in range(CT_DEV):
        own = own_ref[pl.ds(k * SIDE, SIDE)]
        other = [msg_ref[pl.ds(start + i * count + k * SIDE, SIDE)] for i in range(2)]
        for i, value in enumerate((own, jnp.concatenate(other, axis=1))):
            high, low = split(value)
            out_ref[i * CT_DEV + k, pl.ds(0, SIDE)] = high
            out_ref[i * CT_DEV + k, pl.ds(SIDE, SIDE)] = high
            out_ref[i * CT_DEV + k, pl.ds(2 * SIDE, SIDE)] = low


def stack(own, msg):
    shape = jax.ShapeDtypeStruct((2 * CT_DEV, DEPTH, WIDTH), BF16)
    return on_chip(stack_kernel, "stack", (), (own, msg), shape, size=3 << 20)


def range_kernel(first, note_ref, here_ref, stack_ref, *refs):
    msg_refs, out_refs, turned_ref = refs[: -NX - 1], refs[-NX - 1 : -1], refs[-1]
    for ref in out_refs:
        ref[...] = jnp.zeros_like(ref)

    def multiply(k, msg_ref, i, z):
        note = note_ref[source(here_ref, k) * 8 + z]
        place = jnp.maximum(note, 0)
        col = k % 2 * CT_DEV + (place + here_ref[0]) % CT_DEV
        rows = []
        for s in range(NX):
            start = i * SIDE + (here_ref[2] + s) % NX * PART
            rows.append(msg_ref[pl.ds(pl.multiple_of(start, PART), PART)])
        tile = jnp.where(note >= 0, jnp.concatenate(rows), 0.0)
        high, low = split(tile)
        left = jnp.concatenate([high, low, high], axis=1)
        product = jnp.dot(left, stack_ref[col], preferred_element_type=F32)
        for s, ref in enumerate(out_refs):
            ref[i, place // CT_DEV] += product[s * PART : (s + 1) * PART]
        high, low = split(msg_ref[pl.ds(pl.multiple_of(i * SIDE, SIDE), SIDE)].T)
        turned_ref[k, i, :, pl.ds(0, SIDE)] = high
        turned_ref[k, i, :, pl.ds(SIDE, SIDE)] = low

    if first:

        @pl.loop(0, 8)
        def _(k):
            for z in range(SPLIT):
                multiply(k, msg_refs[0].at[source(here_ref, k)], z, z)

    else:

        @pl.loop(0, 8 - SPLIT)
        def _(i):
            for k, msg_ref in enumerate(msg_refs):
                multiply(k, msg_ref, i, i + SPLIT)


def range_part(lanes, notes, here, msgs, weights):
    shape = [jax.ShapeDtypeStruct((len(lanes), 2, PART, WIDTH), F32)] * NX
    shape += [jax.ShapeDtypeStruct((8, len(lanes), SIDE, 2 * SIDE), BF16)]
    kernel = functools.partial(range_kernel, 0 in lanes)
    return on_chip(kernel, "range_part", (notes, here), (weights, *msgs), shape, size=1 << 22)


def corange_kernel(note_ref, here_ref, *refs):
    turned_refs, block_refs, (*out_refs, stack_ref) = refs[:2], refs[2:18], refs[18:]

    for i, ref in enumerate(block_refs):
        z = (here_ref[3] + i) % 8
        for pair in range(2):
            part = (here_ref[2] + i // 8 * 2 + pair) % NX * PART
            high, low = split(ref[pair])
            for r in range(2):
                for j, value in enumerate((high, high, low)):
                    spot = pl.ds(pl.multiple_of(j * SIDE + part, PART), PART)
                    stack_ref[z * 2 + r, spot] = value[r * PART : (r + 1) * PART]

    for ref in out_refs:
        ref[...] = jnp.zeros_like(ref)

    @pl.loop(0, 4)
    def _(step):
        for core, ref in enumerate(out_refs):
            k = step * 2 + core
            spot = source(here_ref, k)
            for z in range(8):
                note = note_ref[spot * 8 + z]
                place = jnp.maximum(note, 0)
                pair = turned_refs[0][k, z] if z < SPLIT else turned_refs[1][k, z - SPLIT]
                pair = jnp.where(note >= 0, pair, jnp.zeros((), BF16))
                left = jnp.concatenate([pair, pair[:, :SIDE]], axis=1)
                right = stack_ref[z * 2 + place // CT_DEV]
                ref[place % CT_DEV] += jnp.dot(left, right, preferred_element_type=F32)


def corange_part(notes, here, turned, near):
    shape = [jax.ShapeDtypeStruct((CT_DEV, SIDE, WIDTH), F32)] * 2
    scratch = [pltpu.VMEM((16, DEPTH, WIDTH), BF16)]
    arrays = (*turned, *near)
    return on_chip(corange_kernel, "corange_part", (notes, here), arrays, shape, scratch, size=1 << 22)


def gather_sum_kernel(in_ref, out_ref):
    total = in_ref[0]
    for k in range(1, 8):
        total = total + in_ref[k]
    out_ref[...] = total


def gather_sum(parts):
    shape = jax.ShapeDtypeStruct(parts.shape[1:], F32)
    return on_chip(gather_sum_kernel, "gather_sum", (), (parts,), shape)


def join_kernel(a_ref, b_ref, *out_refs):
    for k, ref in enumerate(out_refs):
        ref[...] = a_ref[k] + b_ref[k]


def join(a, b):
    shape = [jax.ShapeDtypeStruct((SIDE, WIDTH), F32)] * CT_DEV
    return on_chip(join_kernel, "join", (), (a, b), shape)


def place_kernel(here_ref, *refs):
    *in_refs, out_ref = refs
    for s, ref in enumerate(in_refs):
        out_ref[(here_ref[0] - s + 4) % 4] = ref[...]


def place(here, *arrays):
    shape = jax.ShapeDtypeStruct((4,) + arrays[0].shape, F32)
    return on_chip(place_kernel, "place", (here,), arrays, shape)


def exchange(value, axes):
    return lax.all_to_all(value, axes, split_axis=0, concat_axis=0, tiled=True)


def shifted(value, axis, step):
    n = lax.axis_size(axis)
    return lax.ppermute(value, axis, [(i, (i + step) % n) for i in range(n)])


def partner(value, k):
    pairs = []
    for i in range(8):
        pairs.append((i, (i // 2 + k // 2) % 4 * 2 + (i + k) % 2))
    return lax.ppermute(value, ("y", "c"), pairs)


def settle_kernel(here_ref, *refs):
    *in_refs, out_ref = refs
    for s, ref in enumerate(in_refs):
        x = (here_ref[2] + s) % NX
        for r in range(2):
            spot = pl.ds(pl.multiple_of(r * SIDE + x * PART, PART), PART)
            out_ref[spot] = ref[pl.ds(r * PART, PART)]


def settle(here, pieces):
    shape = jax.ShapeDtypeStruct((2 * SIDE, WIDTH), F32)
    return on_chip(settle_kernel, "settle", (here,), pieces, shape)


def choose_kernel(here_ref, *refs):
    *in_refs, out_ref = refs
    for s, ref in enumerate(in_refs):

        @pl.when((here_ref[0] - here_ref[2] + 4) % 4 == s)
        def _():
            out_ref[...] = ref[...]


def choose(here, arrays):
    shape = jax.ShapeDtypeStruct((2 * SIDE, WIDTH), F32)
    return on_chip(choose_kernel, "choose", (here,), arrays, shape)


def on_device(tiles, tile_dest, tile_row, tile_col, omega, col_scale):
    here = jnp.stack([lax.axis_index(name) for name in "ycxz"]).astype(jnp.int32)
    weights = col_scale.astype(F32)

    index = tile_dest[0, 0, :, 0] * 8 + tile_row[0, 0] * 4 + tile_col[0, 0]
    scaled = omega * weights[:, None]
    first = exchange(pack_first(here, index, tiles[0, 0]), ("y", "c"))
    second = pack_second(here, index, tiles[0, 0], scaled)
    for k in range(1, 8):
        second[k] = partner(second[k], k)
    stacked = stack(scaled, second[1])
    notes = first[:, SPLIT * SIDE, :8].reshape(64)
    notes = notes.astype(jnp.int32)
    parts = []
    turned = []
    for lanes, msgs in ((range(SPLIT), (first,)), (range(SPLIT, 8), second)):
        *blocks, back = range_part(lanes, notes, here, msgs, stacked)
        turned.append(back)
        if parts:
            *blocks, parts[0] = lax.optimization_barrier((*blocks, parts[0]))
        part = blocks[0]
        for s in range(1, NX):
            part = part + shifted(blocks[s], "x", s)
        parts.append(part)
    part = jnp.concatenate(parts)
    piece = gather_sum(exchange(part.reshape(8, HALF, WIDTH), "z"))

    around = [piece] + [shifted(piece, "x", -s) for s in range(1, NX)]
    lane = [settle(here, around)]
    for s in range(1, 4):
        pairs = [(x * 4 + x, (x + s) % 4 * 4 + x) for x in range(4)]
        lane.append(lax.ppermute(lane[0], ("y", "x"), pairs))
    blocks = []
    for pair, up, down in ((around[:2], 4, 3), (around[2:], 3, 4)):
        block = jnp.stack(pair)
        ring = {0: block}
        for step in range(1, 5):
            if step <= up:
                ring[8 - step] = shifted(ring[(9 - step) % 8], "z", 1)
            if step <= down:
                ring[step] = shifted(ring[step - 1], "z", -1)
        blocks += [ring[k] for k in range(8)]

    blocks[4], *lane[1:] = lax.optimization_barrier((blocks[4], *lane[1:]))
    own, other = corange_part(notes, here, turned, blocks)
    total = join(own, shifted(other, "c", 1))
    columns = total[0]
    for s in range(1, 4):
        columns = columns + shifted(total[s], "y", s)
    columns = columns * lax.dynamic_slice_in_dim(weights, here[0] * SIDE, SIDE, axis=0)[:, None]
    corange_local = place(here, columns, *[shifted(columns, "y", s) for s in range(1, 4)])
    corange_local = corange_local.reshape(CT_DEV * SIDE, WIDTH)
    return choose(here, lane), corange_local


def solution(mesh):
    fine = Mesh(mesh.devices.reshape(4, 8, 4, 2), ("y", "z", "x", "c"))
    lane = ("z", "x", "c")
    placed = (
        P("y", lane, None, None, None),
        P("y", lane, None, None),
        P("y", lane, None),
        P("y", lane, None),
        P(lane, None),
        P(lane),
    )
    return jax.shard_map(
        on_device,
        mesh=fine,
        in_specs=placed,
        out_specs=(P(lane, None), P(lane, None)),
        check_vma=False,
    )
```

```python
import functools

import jax
import jax.numpy as jnp
from jax import lax
from jax.experimental import pallas as pl
from jax.experimental.pallas import tpu as pltpu
from jax.sharding import Mesh, PartitionSpec as P

SIDE = 128
WIDTH = 256
CT_DEV = 4
NX = 4
DEPTH = 3 * SIDE
PART = SIDE // 4
HALF = SIDE // 2
SPLIT = 5
VMEM = 6 * 1024 * 1024
F32 = jnp.float32
BF16 = jnp.bfloat16


def split(value):
    high = value.astype(BF16)
    low = (value - high.astype(F32)).astype(BF16)
    return high, low


def params():
    return pltpu.CompilerParams(vmem_limit_bytes=VMEM)


def cost(flops, size):
    return pl.CostEstimate(flops=flops, bytes_accessed=size, transcendentals=0)


def on_chip(kernel, name, scalars, arrays, out_shape, scratch=(), flops=1 << 20, size=1 << 20):
    many = isinstance(out_shape, list)
    vmem, smem = (pl.BlockSpec(memory_space=space) for space in (pltpu.VMEM, pltpu.SMEM))
    return pl.pallas_call(
        kernel,
        out_shape=out_shape,
        in_specs=[smem] * len(scalars) + [vmem] * len(arrays),
        out_specs=[vmem] * len(out_shape) if many else vmem,
        scratch_shapes=list(scratch),
        compiler_params=params(),
        cost_estimate=cost(flops, size),
        name=name,
    )(*scalars, *arrays)


def source(here_ref, k):
    return (here_ref[0] - k // 2 + 4) % 4 * 2 + (here_ref[1] + k) % 2


def find_tiles(here_ref, index_ref, from_ref, note_ref):
    for i in range(64):
        from_ref[i] = 0
        if note_ref is not None:
            note_ref[i] = -1

    @pl.loop(0, index_ref.shape[0])
    def _(t):
        index = index_ref[t]
        lane = index // 8
        z, x, c = lane // 8, lane // 2 % 4, lane % 2
        k = (x - here_ref[0] + 4) % 4 * 2 + (c + here_ref[1]) % 2
        slot = k * 8 + z
        from_ref[slot] = t
        if note_ref is not None:
            note_ref[slot] = index // 4 % 2 * CT_DEV + (index - x + 64) % 4


def first_kernel(here_ref, index_ref, tiles_ref, out_ref, from_ref, note_ref):
    find_tiles(here_ref, index_ref, from_ref, note_ref)
    spot = lax.broadcasted_iota(jnp.int32, (8, SIDE), 1)

    @pl.loop(0, 8)
    def _(k):
        ref = out_ref.at[(here_ref[0] + k // 2) % 4 * 2 + (here_ref[1] + k) % 2]
        notes = jnp.full((8, SIDE), -1, jnp.int32)
        for z in range(8):
            if z < SPLIT:
                ref[pl.ds(z * SIDE, SIDE)] = tiles_ref[from_ref[k * 8 + z]]
            notes = jnp.where(spot == z, note_ref[k * 8 + z], notes)
        ref[pl.ds(SPLIT * SIDE, 8)] = notes.astype(F32)


def pack_first(here, index, tiles):
    shape = jax.ShapeDtypeStruct((8, SPLIT * SIDE + 8, SIDE), F32)
    scratch = [pltpu.SMEM((64,), jnp.int32)] * 2
    return on_chip(first_kernel, "pack_first", (here, index), (tiles,), shape, scratch)


def second_kernel(here_ref, index_ref, tiles_ref, omega_ref, *refs):
    out_refs, from_ref = refs[:-1], refs[-1]
    find_tiles(here_ref, index_ref, from_ref, None)

    @pl.loop(0, 8 - SPLIT)
    def _(i):
        for k, ref in enumerate(out_refs):
            start = pl.multiple_of(i * SIDE, SIDE)
            ref[pl.ds(start, SIDE)] = tiles_ref[from_ref[k * 8 + SPLIT + i]]

    start, count = (8 - SPLIT) * SIDE, CT_DEV * SIDE
    out_refs[1][pl.ds(start, count)] = omega_ref[:, pl.ds(0, SIDE)]
    out_refs[1][pl.ds(start + count, count)] = omega_ref[:, pl.ds(SIDE, SIDE)]


def pack_second(here, index, tiles, omega):
    rows = [(8 - SPLIT) * SIDE] * 8
    rows[1] += 2 * CT_DEV * SIDE
    shape = [jax.ShapeDtypeStruct((count, SIDE), F32) for count in rows]
    scratch = [pltpu.SMEM((64,), jnp.int32)]
    arrays = (tiles, omega)
    return list(on_chip(second_kernel, "pack_second", (here, index), arrays, shape, scratch))


def stack_kernel(own_ref, msg_ref, out_ref):
    start, count = (8 - SPLIT) * SIDE, CT_DEV * SIDE
    for k in range(CT_DEV):
        own = own_ref[pl.ds(k * SIDE, SIDE)]
        other = [msg_ref[pl.ds(start + i * count + k * SIDE, SIDE)] for i in range(2)]
        for i, value in enumerate((own, jnp.concatenate(other, axis=1))):
            high, low = split(value)
            out_ref[i * CT_DEV + k, pl.ds(0, SIDE)] = high
            out_ref[i * CT_DEV + k, pl.ds(SIDE, SIDE)] = high
            out_ref[i * CT_DEV + k, pl.ds(2 * SIDE, SIDE)] = low


def stack(own, msg):
    shape = jax.ShapeDtypeStruct((2 * CT_DEV, DEPTH, WIDTH), BF16)
    return on_chip(stack_kernel, "stack", (), (own, msg), shape, size=3 << 20)


def range_kernel(first, note_ref, here_ref, stack_ref, *refs):
    msg_refs, out_refs, turned_ref = refs[: -NX - 1], refs[-NX - 1 : -1], refs[-1]
    for ref in out_refs:
        ref[...] = jnp.zeros_like(ref)

    def multiply(k, msg_ref, i, z):
        note = note_ref[source(here_ref, k) * 8 + z]
        place = jnp.maximum(note, 0)
        col = k % 2 * CT_DEV + (place + here_ref[0]) % CT_DEV
        rows = []
        for s in range(NX):
            start = i * SIDE + (here_ref[2] + s) % NX * PART
            rows.append(msg_ref[pl.ds(pl.multiple_of(start, PART), PART)])
        tile = jnp.where(note >= 0, jnp.concatenate(rows), 0.0)
        high, low = split(tile)
        left = jnp.concatenate([high, low, high], axis=1)
        product = jnp.dot(left, stack_ref[col], preferred_element_type=F32)
        for s, ref in enumerate(out_refs):
            ref[i, place // CT_DEV] += product[s * PART : (s + 1) * PART]
        high, low = split(msg_ref[pl.ds(pl.multiple_of(i * SIDE, SIDE), SIDE)].T)
        turned_ref[k, i, :, pl.ds(0, SIDE)] = high
        turned_ref[k, i, :, pl.ds(SIDE, SIDE)] = low

    if first:

        @pl.loop(0, 8)
        def _(k):
            for z in range(SPLIT):
                multiply(k, msg_refs[0].at[source(here_ref, k)], z, z)

    else:

        @pl.loop(0, 8 - SPLIT)
        def _(i):
            for k, msg_ref in enumerate(msg_refs):
                multiply(k, msg_ref, i, i + SPLIT)


def range_part(lanes, notes, here, msgs, weights):
    shape = [jax.ShapeDtypeStruct((len(lanes), 2, PART, WIDTH), F32)] * NX
    shape += [jax.ShapeDtypeStruct((8, len(lanes), SIDE, 2 * SIDE), BF16)]
    kernel = functools.partial(range_kernel, 0 in lanes)
    return on_chip(kernel, "range_part", (notes, here), (weights, *msgs), shape, size=1 << 22)


def corange_kernel(note_ref, here_ref, *refs):
    turned_refs, block_refs, (*out_refs, stack_ref) = refs[:2], refs[2:18], refs[18:]

    for i, ref in enumerate(block_refs):
        z = (here_ref[3] + i) % 8
        for pair in range(2):
            part = (here_ref[2] + i // 8 * 2 + pair) % NX * PART
            high, low = split(ref[pair])
            for r in range(2):
                for j, value in enumerate((high, high, low)):
                    spot = pl.ds(pl.multiple_of(j * SIDE + part, PART), PART)
                    stack_ref[z * 2 + r, spot] = value[r * PART : (r + 1) * PART]

    for ref in out_refs:
        ref[...] = jnp.zeros_like(ref)

    @pl.loop(0, 4)
    def _(step):
        for core, ref in enumerate(out_refs):
            k = step * 2 + core
            spot = source(here_ref, k)
            for z in range(8):
                note = note_ref[spot * 8 + z]
                place = jnp.maximum(note, 0)
                pair = turned_refs[0][k, z] if z < SPLIT else turned_refs[1][k, z - SPLIT]
                pair = jnp.where(note >= 0, pair, jnp.zeros((), BF16))
                left = jnp.concatenate([pair, pair[:, :SIDE]], axis=1)
                right = stack_ref[z * 2 + place // CT_DEV]
                ref[place % CT_DEV] += jnp.dot(left, right, preferred_element_type=F32)


def corange_part(notes, here, turned, near):
    shape = [jax.ShapeDtypeStruct((CT_DEV, SIDE, WIDTH), F32)] * 2
    scratch = [pltpu.VMEM((16, DEPTH, WIDTH), BF16)]
    arrays = (*turned, *near)
    return on_chip(corange_kernel, "corange_part", (notes, here), arrays, shape, scratch, size=1 << 22)


def gather_sum_kernel(in_ref, out_ref):
    total = in_ref[0]
    for k in range(1, 8):
        total = total + in_ref[k]
    out_ref[...] = total


def gather_sum(parts):
    shape = jax.ShapeDtypeStruct(parts.shape[1:], F32)
    return on_chip(gather_sum_kernel, "gather_sum", (), (parts,), shape)


def join_kernel(a_ref, b_ref, *out_refs):
    for k, ref in enumerate(out_refs):
        ref[...] = a_ref[k] + b_ref[k]


def join(a, b):
    shape = [jax.ShapeDtypeStruct((SIDE, WIDTH), F32)] * CT_DEV
    return on_chip(join_kernel, "join", (), (a, b), shape)


def place_kernel(here_ref, *refs):
    *in_refs, out_ref = refs
    for s, ref in enumerate(in_refs):
        out_ref[(here_ref[0] - s + 4) % 4] = ref[...]


def place(here, *arrays):
    shape = jax.ShapeDtypeStruct((4,) + arrays[0].shape, F32)
    return on_chip(place_kernel, "place", (here,), arrays, shape)


def exchange(value, axes):
    return lax.all_to_all(value, axes, split_axis=0, concat_axis=0, tiled=True)


def shifted(value, axis, step):
    n = lax.axis_size(axis)
    return lax.ppermute(value, axis, [(i, (i + step) % n) for i in range(n)])


def partner(value, k):
    pairs = []
    for i in range(8):
        pairs.append((i, (i // 2 + k // 2) % 4 * 2 + (i + k) % 2))
    return lax.ppermute(value, ("y", "c"), pairs)


def settle_kernel(here_ref, *refs):
    *in_refs, out_ref = refs
    for s, ref in enumerate(in_refs):
        x = (here_ref[2] + s) % NX
        for r in range(2):
            spot = pl.ds(pl.multiple_of(r * SIDE + x * PART, PART), PART)
            out_ref[spot] = ref[pl.ds(r * PART, PART)]


def settle(here, pieces):
    shape = jax.ShapeDtypeStruct((2 * SIDE, WIDTH), F32)
    return on_chip(settle_kernel, "settle", (here,), pieces, shape)


def choose_kernel(here_ref, *refs):
    *in_refs, out_ref = refs
    for s, ref in enumerate(in_refs):

        @pl.when((here_ref[0] - here_ref[2] + 4) % 4 == s)
        def _():
            out_ref[...] = ref[...]


def choose(here, arrays):
    shape = jax.ShapeDtypeStruct((2 * SIDE, WIDTH), F32)
    return on_chip(choose_kernel, "choose", (here,), arrays, shape)


def on_device(tiles, tile_dest, tile_row, tile_col, omega, col_scale):
    here = jnp.stack([lax.axis_index(name) for name in "ycxz"]).astype(jnp.int32)
    weights = col_scale.astype(F32)

    index = tile_dest[0, 0, :, 0] * 8 + tile_row[0, 0] * 4 + tile_col[0, 0]
    scaled = omega * weights[:, None]
    first = exchange(pack_first(here, index, tiles[0, 0]), ("y", "c"))
    second = pack_second(here, index, tiles[0, 0], scaled)
    for k in range(1, 8):
        second[k] = partner(second[k], k)
    stacked = stack(scaled, second[1])
    notes = first[:, SPLIT * SIDE, :8].reshape(64)
    notes = notes.astype(jnp.int32)
    parts = []
    turned = []
    for lanes, msgs in ((range(SPLIT), (first,)), (range(SPLIT, 8), second)):
        *blocks, back = range_part(lanes, notes, here, msgs, stacked)
        turned.append(back)
        if parts:
            *blocks, parts[0] = lax.optimization_barrier((*blocks, parts[0]))
        part = blocks[0]
        for s in range(1, NX):
            part = part + shifted(blocks[s], "x", s)
        parts.append(part)
    part = jnp.concatenate(parts)
    piece = gather_sum(exchange(part.reshape(8, HALF, WIDTH), "z"))

    around = [piece] + [shifted(piece, "x", -s) for s in range(1, NX)]
    lane = [settle(here, around)]
    for s in range(1, 4):
        pairs = [(x * 4 + x, (x + s) % 4 * 4 + x) for x in range(4)]
        lane.append(lax.ppermute(lane[0], ("y", "x"), pairs))
    blocks = []
    for pair, up, down in ((around[:2], 4, 3), (around[2:], 3, 4)):
        block = jnp.stack(pair)
        ring = {0: block}
        for step in range(1, 5):
            if step <= up:
                ring[8 - step] = shifted(ring[(9 - step) % 8], "z", 1)
            if step <= down:
                ring[step] = shifted(ring[step - 1], "z", -1)
        blocks += [ring[k] for k in range(8)]

    blocks[4], *lane[1:] = lax.optimization_barrier((blocks[4], *lane[1:]))
    own, other = corange_part(notes, here, turned, blocks)
    total = join(own, shifted(other, "c", 1))
    columns = total[0]
    for s in range(1, 4):
        columns = columns + shifted(total[s], "y", s)
    columns = columns * lax.dynamic_slice_in_dim(weights, here[0] * SIDE, SIDE, axis=0)[:, None]
    corange_local = place(here, columns, *[shifted(columns, "y", s) for s in range(1, 4)])
    corange_local = corange_local.reshape(CT_DEV * SIDE, WIDTH)
    return choose(here, lane), corange_local


def solution(mesh):
    fine = Mesh(mesh.devices.reshape(4, 8, 4, 2), ("y", "z", "x", "c"))
    lane = ("z", "x", "c")
    placed = (
        P("y", lane, None, None, None),
        P("y", lane, None, None),
        P("y", lane, None),
        P("y", lane, None),
        P(lane, None),
        P(lane),
    )
    return jax.shard_map(
        on_device,
        mesh=fine,
        in_specs=placed,
        out_specs=(P(lane, None), P(lane, None)),
        check_vma=False,
    )
```
